256 devices in a mesh: dp: 64 (over z, y, core), fsdp: 4 (over x).
Axes of the slice: x: 4, y: 4, z: 8, core: 2. Of those that a mesh axis runs over, the one named last changes fastest.
Arguments:
- x_rows: bfloat16 [4, 8192, 1024], P('fsdp', 'dp'), may hold values from -6 to 6
- cotangent: bfloat16 [4, 16384, 1024], P('fsdp', 'dp'), may hold values from -6 to 6
- w_in: bfloat16 [1024, 2048], P('fsdp'), may hold values from -0.1875 to 0.1875
- w_out: bfloat16 [512, 1024], P('fsdp'), may hold values from -0.5 to 0.5
- hist_blocks: int32 [4, 64], P('fsdp'), may hold values from 1 to 4, as said below
- owner: int32 [4, 64], P('fsdp'), may hold values from 0 to 63, as said below
Outputs:
- layer_out: bfloat16 [4, 16384, 1024], P('fsdp', 'dp')
- grad_x: bfloat16 [4, 8192, 1024], P('fsdp', 'dp')
- grad_w_in: float32 [1024, 2048], P('fsdp')
- grad_w_out: float32 [512, 1024], P('fsdp')
The draws below stay inside these ranges and needn't reach their ends.
Inputs may be any that keep to these rules, and one draw needn't show every extreme that they name: `hist_blocks`: in each group the blocks of all histories sum to 128, and some history has exactly 4 blocks. In each group the histories of one owner have at most 4 blocks together, and some owner has exactly 4.
All inputs are finite; a program needn't handle non-finite values.
Results may differ from the reference program's by a relative error of at most 0.022.
Values may be sent and summed in bfloat16 or wider, within the bound.
No kernel may reach another device: no remote copies, remote signals or barrier semaphores. Data moves between devices by JAX's collectives and lax.ppermute only.
A program may use at most 128 MiB of HBM per device.

```python
import jax
import jax.numpy as jnp
from jax import lax

D = 1024
HEAD = 128
TOK_DEV = 128
E = 512
NSEQ = 64
OWN_ROWS = 256
SLOT = 4
GROUPS = 4
ROWS = 8192
OWNED = 16384
N_DP = 64


def shared_blocks(key):

    def one_group(group):
        group_key = jax.random.fold_in(key, group)
        base = jnp.ones((NSEQ,), jnp.int32).at[0].set(SLOT)
        prefer = jax.random.randint(jax.random.fold_in(group_key, 1), (NSEQ,), 1, 5)
        prefer = (prefer * prefer).astype(jnp.int32)
        order_ids = jnp.arange(NSEQ, dtype=jnp.int32)

        def grow(step, current):
            picks = jax.random.randint(jax.random.fold_in(group_key, step + 100), (NSEQ,), 0, 4096)
            score = picks * prefer * NSEQ + order_ids
            score = jnp.where(current < SLOT, score, -1)
            chosen = jnp.argmax(score)
            return current.at[chosen].add(1)
        filled = lax.fori_loop(0, TOK_DEV - NSEQ - SLOT + 1, grow, base)
        shuffle = jax.random.permutation(jax.random.fold_in(group_key, 2), NSEQ)
        return filled[shuffle].astype(jnp.int32)
    return jax.vmap(one_group)(jnp.arange(GROUPS, dtype=jnp.int32))


def draw_hist_blocks(key, part):
    return shared_blocks(key)


def draw_owner(key, part):
    blocks = shared_blocks(key)
    key = jax.random.fold_in(key, 3)

    def one_group(group, sizes):
        group_key = jax.random.fold_in(key, group)
        cost = sizes * sizes
        ties = jax.random.permutation(jax.random.fold_in(group_key, 1), NSEQ).astype(jnp.int32)
        order = jnp.argsort(-(cost * NSEQ + ties))
        owner_ties = jax.random.permutation(jax.random.fold_in(group_key, 2), N_DP).astype(jnp.int32)

        def place(step, state):
            load_cost, load_rows, owners = state
            item = order[step]
            size = sizes[item]
            score = jnp.where(load_rows + size <= SLOT, load_cost * N_DP + owner_ties, 2 ** 30)
            target = jnp.argmin(score).astype(jnp.int32)
            return (load_cost.at[target].add(size * size), load_rows.at[target].add(size), owners.at[item].set(target))
        start_state = (jnp.zeros((N_DP,), jnp.int32), jnp.zeros((N_DP,), jnp.int32), jnp.zeros((NSEQ,), jnp.int32))
        return lax.fori_loop(0, NSEQ, place, start_state)[2]
    return jax.vmap(one_group)(jnp.arange(GROUPS, dtype=jnp.int32), blocks)


def steps_of(stream_key, shape, split, least, largest):
    factor_of = 1.0
    for position, blocks in split:
        draws = jax.random.uniform(jax.random.fold_in(jax.random.fold_in(stream_key, 6), position), (blocks,), jnp.float32, least / len(split), largest / len(split))
        factor_of = factor_of * jnp.repeat(jnp.exp(draws), shape[position] // blocks).reshape((-1,) + (1,) * (len(shape) - 1 - position))
    return factor_of


def scatter_about(rng, shape, scale, bound, cuts=(), kind=jnp.bfloat16):
    array = scale * jax.random.normal(rng, shape, jnp.float32)
    if cuts:
        array = array * steps_of(rng, shape, cuts, -0.22, 0.18)
    return jnp.clip(array, -bound, bound).astype(kind)


def setup_inputs(seed: int = 0) -> dict:
    seeds = jax.random.split(jax.random.key(seed), 7)
    return {
        "x_rows": scatter_about(seeds[0], (GROUPS, ROWS, D), 1.0, 6.0, ((0, 4), (1, 64))),
        "cotangent": scatter_about(seeds[1], (GROUPS, OWNED, D), 1.0, 6.0, ((0, 4), (1, 64))),
        "w_in": scatter_about(seeds[2], (D, 4 * E), D ** -0.5, 0.1875, ((0, 4),)),
        "w_out": scatter_about(seeds[3], (E, D), (E // 4) ** -0.5, 0.5, ((0, 4),)),
        "hist_blocks": draw_hist_blocks(jax.random.fold_in(seeds[6], 71), 0),
        "owner": draw_owner(jax.random.fold_in(seeds[6], 71), 0),
    }


epsilon = 1e-06

def layer_rows(rows_in, w_in, w_out, segment):
    capacity = rows_in.shape[0]
    width = w_out.shape[0]
    values = rows_in.astype(jnp.float32)
    centred = values - lax.optimization_barrier(jnp.mean(values, axis=1, keepdims=True))
    spread = lax.optimization_barrier(jnp.mean(centred * centred, axis=1, keepdims=True))
    normed = (centred * lax.rsqrt(spread + epsilon)).astype(jnp.bfloat16)
    active = jax.nn.silu(jnp.dot(normed, w_in, preferred_element_type=jnp.float32)).astype(jnp.bfloat16)
    gate_u = active[:, :width]
    value_v = active[:, width:2 * width]
    query = active[:, 2 * width:3 * width]
    key_k = active[:, 3 * width:]
    positions = jnp.arange(capacity, dtype=jnp.int32)
    visible = (segment[:, None] == segment[None, :]) & (positions[None, :] <= positions[:, None]) & (segment[:, None] >= 0)
    pieces = []
    for head in range(width // HEAD):
        first = head * HEAD
        scores = lax.dot_general(query[:, first:first + HEAD], key_k[:, first:first + HEAD], (((1,), (1,)), ((), ())), preferred_element_type=jnp.float32) * HEAD ** (-0.5)
        weights = jnp.where(visible, jax.nn.silu(scores) / capacity, 0.0).astype(jnp.bfloat16)
        pieces.append(jnp.dot(weights, value_v[:, first:first + HEAD], preferred_element_type=jnp.float32))
    attended = jnp.concatenate(pieces, axis=1)
    att_centred = attended - lax.optimization_barrier(jnp.mean(attended, axis=1, keepdims=True))
    att_spread = lax.optimization_barrier(jnp.mean(att_centred * att_centred, axis=1, keepdims=True))
    mixed = (gate_u.astype(jnp.float32) * (att_centred * lax.rsqrt(att_spread + epsilon))).astype(jnp.bfloat16)
    return (jnp.dot(mixed, w_out, preferred_element_type=jnp.float32) + values).astype(jnp.bfloat16)

def history_layout(blocks, owners):
    count = blocks.shape[0]
    start = (jnp.cumsum(blocks) - blocks).astype(jnp.int32)
    order_ids = jnp.arange(count, dtype=jnp.int32)
    earlier = (owners[:, None] == owners[None, :]) & (order_ids[None, :] < order_ids[:, None])
    before = lax.optimization_barrier(jnp.sum(jnp.where(earlier, blocks[None, :], 0), axis=1)).astype(jnp.int32)
    return (start, before)

def anchor_targets(start, before, row_count):
    row_ids = jnp.arange(row_count, dtype=jnp.int32)
    seq_of = (lax.optimization_barrier(jnp.sum((start[None, :] <= row_ids[:, None]).astype(jnp.int32), axis=1)) - 1).astype(jnp.int32)
    slot_index = (before[seq_of] + row_ids - start[seq_of]).astype(jnp.int32)
    return (seq_of, slot_index)

def owner_segment(blocks, owners, before, my_index, capacity, devices):
    count = blocks.shape[0]
    row_ids = jnp.arange(capacity, dtype=jnp.int32)[:, None]
    inside = (owners[None, :] == my_index) & (row_ids >= before[None, :] * devices) & (row_ids < (before + blocks)[None, :] * devices)
    labels = jnp.arange(count, dtype=jnp.int32)[None, :] + 1
    return (lax.optimization_barrier(jnp.sum(jnp.where(inside, labels, 0), axis=1)) - 1).astype(jnp.int32)

def reference(x_rows, cotangent, w_in, w_out, hist_blocks, owner):
    total_in = jnp.zeros(w_in.shape, jnp.float32)
    total_out = jnp.zeros(w_out.shape, jnp.float32)
    outputs = []
    grads = []
    for group in range(GROUPS):
        blocks = hist_blocks[group]
        owners = owner[group]
        start, before = history_layout(blocks, owners)
        seq_of, slot_index = anchor_targets(start, before, TOK_DEV)
        all_rows = jnp.arange(ROWS, dtype=jnp.int32)
        source = (all_rows // TOK_DEV).astype(jnp.int32)
        local = (all_rows % TOK_DEV).astype(jnp.int32)
        target = (owners[seq_of[local]] * OWN_ROWS + slot_index[local] * N_DP + source).astype(jnp.int32)
        owned = jnp.zeros((OWNED, D), jnp.bfloat16).at[target].set(x_rows[group])
        cot_group = cotangent[group]

        def per_owner(carry, index):
            rows_in = lax.dynamic_slice_in_dim(owned, index * OWN_ROWS, OWN_ROWS, 0)
            cot_rows = lax.dynamic_slice_in_dim(cot_group, index * OWN_ROWS, OWN_ROWS, 0)
            segment = owner_segment(blocks, owners, before, index, OWN_ROWS, N_DP)
            result, pullback = jax.vjp(lambda first_arg, second_arg, third_arg: layer_rows(first_arg, second_arg, third_arg, segment), rows_in, w_in, w_out)
            d_rows, d_in, d_out = pullback(cot_rows)
            return ((carry[0] + d_in.astype(jnp.float32), carry[1] + d_out.astype(jnp.float32)), (result, d_rows))
        (total_in, total_out), (results, d_owned) = lax.scan(per_owner, (total_in, total_out), jnp.arange(N_DP, dtype=jnp.int32))
        outputs.append(results.reshape(OWNED, D))
        grads.append(d_owned.reshape(OWNED, D)[target])
    factor = 1.0 / (GROUPS * N_DP)
    return (jnp.stack(outputs), jnp.stack(grads), total_in * factor, total_out * factor)
```

```python
import functools

import jax
import jax.numpy as jnp
from jax import lax
from jax.experimental import pallas as pl
from jax.experimental.pallas import tpu as pltpu
from jax.sharding import Mesh, PartitionSpec as P

F32 = jnp.float32
BF16 = jnp.bfloat16
EPS = 1e-06
HEAD = 128
DP = ("z", "y", "c")
NN = (((1,), (0,)), ((), ()))
NT = (((1,), (1,)), ((), ()))
TN = (((0,), (0,)), ((), ()))
VMEM_LIMIT = 56 * 1024 * 1024


def dot(a, b, dims=NN):
    return lax.dot_general(a, b, dims, preferred_element_type=F32)


def iota(shape, dim):
    return lax.broadcasted_iota(jnp.int32, shape, dim)


def call(body, outs, args, name, scratch=(), smem=0):
    return pl.pallas_call(
        body,
        out_shape=[jax.ShapeDtypeStruct(s, d) for s, d in outs],
        in_specs=[pl.BlockSpec(memory_space=pltpu.VMEM) for _ in args],
        out_specs=[pl.BlockSpec(memory_space=pltpu.VMEM) for _ in outs],
        scratch_shapes=[pltpu.VMEM(s, d) for s, d in scratch],
        compiler_params=pltpu.CompilerParams(vmem_limit_bytes=VMEM_LIMIT),
        name=name,
    )(*args)


def histories(blocks_ref, owners_ref):
    n_row = blocks_ref[...].astype(F32)
    o_row = owners_ref[...].astype(F32)
    count = n_row.shape[1]
    r, c = iota((count, count), 0), iota((count, count), 1)
    column = lambda cond, row: jnp.sum(jnp.where(cond, row, 0.0), axis=1, keepdims=True)
    n_col = column(r == c, n_row)
    o_col = column(r == c, o_row)
    start = column(c < r, n_row)
    same = o_col == o_row
    before_col = column((c < r) & same, n_row)
    before_row = jnp.sum(jnp.where((r < c) & same, n_col, 0.0), axis=0, keepdims=True)
    return n_row, o_row, n_col, o_col, start, before_col, before_row


def slots_of_rows(blocks_ref, owners_ref, count):
    _, _, n_col, o_col, start, before, _ = histories(blocks_ref, owners_ref)
    b = iota((n_col.shape[0], count), 1).astype(F32)
    inside = (start <= b) & (b < start + n_col)
    code = jnp.sum(jnp.where(inside, o_col * 4.0 + before - start, 0.0), axis=0, keepdims=True)
    return (code + b[:1]).astype(jnp.int32)


def prep_body(blocks_ref, owners_ref, x_ref, w_in_ref, w_out_ref, out_ref, pack_ref):
    half = lax.axis_index("c")
    pack_ref[:256, :] = w_in_ref[:, pl.ds(pl.multiple_of(half * 1024, 1024), 1024)]
    wo = w_out_ref[:, pl.ds(pl.multiple_of(half * 512, 512), 512)]
    pack_ref[256:, :512] = wo[:64]
    pack_ref[256:, 512:] = wo[64:]
    code = slots_of_rows(blocks_ref, owners_ref, 128)
    row = iota((1024, 128), 0)
    total = None
    for j in range(4):
        pick = (row == code * 4 + j).astype(F32).astype(BF16)
        part = dot(pick, x_ref[:, j * 256 : (j + 1) * 256])
        total = part if total is None else total + part
    out_ref[...] = total.astype(BF16)


def rows_back_body(blocks_ref, owners_ref, returned_ref, out_ref):
    code = slots_of_rows(blocks_ref, owners_ref, 128)
    eye = iota((128, 128), 0) == iota((128, 128), 1)
    column = jnp.sum(jnp.where(eye, code.astype(F32), 0.0), axis=1, keepdims=True).astype(jnp.int32)
    lane = iota((128, 1024), 1)
    for j in range(4):
        pick = (lane == column * 4 + j).astype(F32).astype(BF16)
        out_ref[:, j * 256 : (j + 1) * 256] = dot(pick, returned_ref[...]).astype(BF16)


def weights_of(x, half, refs):
    w_in, w_out, own, other = refs
    other_half = 1 - half

    def proj(k, is_own):
        if k == 0:
            h = half if is_own else other_half
            return w_in[:, pl.ds(pl.multiple_of(h * 1024, 1024), 1024)]
        return (own if is_own else other)[k - 1][:256, :]

    def back(k, is_own):
        if k == 0:
            h = half if is_own else other_half
            return w_out[:, pl.ds(pl.multiple_of(h * 512, 512), 512)]
        ref = (own if is_own else other)[k - 1]
        return jnp.concatenate([ref[256:, :512], ref[256:, 512:]], axis=0)

    return proj, back


def grad_chunks(x, y, half, nrm, dpre, mix, cot, out):
    right = cot[:, pl.ds(pl.multiple_of(half * 512, 512), 512)]
    for sx in range(4):
        block = (x + sx) % 4
        d_in = dot(nrm[block], dpre[half], TN).astype(BF16)
        d_out = dot(mix[block], right, TN).astype(BF16)
        tail = jnp.concatenate([d_out[:64], d_out[64:]], axis=1)
        for m in range(4):
            sy = (m + 4 - y) % 4
            if m < 3:
                rows = d_in[80 * m : 80 * m + 80]
            else:
                rows = jnp.concatenate([d_in[240:], tail], axis=0)
            out[0, sx, sy] = rows[:, :512]
            out[1, sy, sx] = rows[:, 512:]


CHUNK = 32


def layer_body(
    blocks_ref, owners_ref, arrived, cot, w_in, w_out, a1, b1, a2, b2, a3, b3,
    layer_out, gother, nrm, dpre, mix, rstd,
    owned, pre, act, att, att_rstd, weights, dscore, dmixed, datt,
):
    x, y, c = lax.axis_index("x"), lax.axis_index("y"), lax.axis_index("c")
    me = (lax.axis_index("z") * 4 + y) * 2 + c
    proj, back = weights_of(x, c, (w_in, w_out, (a1, a2, a3), (b1, b2, b3)))
    halves = ((True, c), (False, 1 - c))

    t = iota((256, 1024), 0)
    wanted = (t & 63) * 16 + (t >> 6) * 4
    lane = iota((256, 1024), 1)
    for j in range(4):
        pick = (lane == wanted + j).astype(F32).astype(BF16)
        owned[:, j * 256 : (j + 1) * 256] = dot(pick, arrived[...])

    def norm_rows(r, _):
        rows = pl.ds(pl.multiple_of(r * CHUNK, CHUNK), CHUNK)
        v = owned[rows, :]
        cen = v - jnp.sum(v, axis=1, keepdims=True) * (1.0 / 1024)
        rs = lax.rsqrt(jnp.sum(cen * cen, axis=1, keepdims=True) * (1.0 / 1024) + EPS)
        n = (cen * rs).astype(BF16)
        for j in range(4):
            nrm[j, rows, :] = n[:, j * 256 : (j + 1) * 256]
        rstd[rows, :] = jnp.broadcast_to(rs, (CHUNK, 128))
        return 0

    lax.fori_loop(0, 256 // CHUNK, norm_rows, 0)

    for is_own, h in halves:
        total = None
        for k in range(4):
            part = dot(nrm[(x + 4 - k) % 4], proj(k, is_own))
            total = part if total is None else total + part
        pre[h] = total

    def activate(r, _):
        rows = pl.ds(pl.multiple_of(r * CHUNK, CHUNK), CHUNK)
        for h in range(2):
            v = pre[h, rows, :]
            sig = jax.nn.sigmoid(v)
            act[h, rows, :] = (v * sig).astype(BF16)
            pre[h, rows, :] = sig * (1.0 + v * (1.0 - sig))
        return 0

    lax.fori_loop(0, 256 // CHUNK, activate, 0)

    n_row, o_row, n_col, o_col, _, before_col, before_row = histories(blocks_ref, owners_ref)
    mine = me.astype(F32)
    label = 1.0 + iota((64, 256), 0).astype(F32)
    at = iota((64, 256), 1).astype(F32)
    inside = (o_col == mine) & (at >= before_col * 64.0) & (at < (before_col + n_col) * 64.0)
    seg_row = jnp.sum(jnp.where(inside, label, 0.0), axis=0, keepdims=True)
    label = 1.0 + iota((256, 64), 1).astype(F32)
    at = iota((256, 64), 0).astype(F32)
    inside = (o_row == mine) & (at >= before_row * 64.0) & (at < (before_row + n_row) * 64.0)
    seg_col = jnp.sum(jnp.where(inside, label, 0.0), axis=1, keepdims=True)
    visible = (seg_row == seg_col) & (iota((256, 256), 1) <= iota((256, 256), 0)) & (seg_col > 0.0)
    mask = jnp.where(visible, 1.0 / 256.0, 0.0)

    scale = HEAD ** (-0.5)
    for h in range(4):
        lo, hi = h * HEAD, (h + 1) * HEAD
        s = dot(act[1, :, lo:hi], act[1, :, 512 + lo : 512 + hi], NT) * scale
        sig = jax.nn.sigmoid(s)
        w = (s * sig * mask).astype(BF16)
        weights[h] = w
        dscore[h] = mask * (sig * (1.0 + s * (1.0 - sig))) * scale
        att[:, lo:hi] = dot(w, act[0, :, 512 + lo : 512 + hi])

    def mix_rows(r, _):
        rows = pl.ds(pl.multiple_of(r * CHUNK, CHUNK), CHUNK)
        v = att[rows, :]
        cen = v - jnp.sum(v, axis=1, keepdims=True) * (1.0 / 512)
        rs = lax.rsqrt(jnp.sum(cen * cen, axis=1, keepdims=True) * (1.0 / 512) + EPS)
        hat = cen * rs
        mixed = (act[0, rows, :512].astype(F32) * hat).astype(BF16)
        for h in range(4):
            mix[h, rows, :] = mixed[:, h * HEAD : (h + 1) * HEAD]
        att[rows, :] = hat
        att_rstd[rows, :] = jnp.broadcast_to(rs, (CHUNK, 128))
        return 0

    lax.fori_loop(0, 256 // CHUNK, mix_rows, 0)

    for is_own, h in halves:
        columns = pl.ds(pl.multiple_of(h * 512, 512), 512)
        total = owned[:, columns]
        for k in range(4):
            total = total + dot(mix[(x + 4 - k) % 4], back(k, is_own))
        layer_out[:, columns] = total.astype(BF16)

    for k in range(4):
        total = None
        for is_own, h in halves:
            columns = pl.ds(pl.multiple_of(h * 512, 512), 512)
            part = dot(cot[:, columns], back(k, is_own), NT)
            total = part if total is None else total + part
        dmixed[(x + 4 - k) % 4] = total.astype(BF16)

    def unmix_rows(r, _):
        rows = pl.ds(pl.multiple_of(r * CHUNK, CHUNK), CHUNK)
        dm = jnp.concatenate([dmixed[h, rows, :] for h in range(4)], axis=1).astype(F32)
        hat = att[rows, :]
        du = (dm * hat).astype(BF16).astype(F32)
        dpre[0, rows, :512] = (du * pre[0, rows, :512]).astype(BF16)
        dh = dm * act[0, rows, :512].astype(F32)
        m1 = jnp.sum(dh, axis=1, keepdims=True) * (1.0 / 512)
        m2 = jnp.sum(dh * hat, axis=1, keepdims=True) * (1.0 / 512)
        datt[rows, :] = (att_rstd[rows, :1] * (dh - m1 - hat * m2)).astype(BF16)
        return 0

    lax.fori_loop(0, 256 // CHUNK, unmix_rows, 0)

    for h in range(4):
        lo, hi = h * HEAD, (h + 1) * HEAD
        d_h = datt[:, lo:hi]
        dw = dot(d_h, act[0, :, 512 + lo : 512 + hi], NT).astype(BF16).astype(F32)
        ds = (dw * dscore[h]).astype(BF16)
        dv = dot(weights[h], d_h, TN).astype(BF16).astype(F32)
        dq = dot(ds, act[1, :, 512 + lo : 512 + hi]).astype(BF16).astype(F32)
        dk = dot(ds, act[1, :, lo:hi], TN).astype(BF16).astype(F32)
        dpre[0, :, 512 + lo : 512 + hi] = (dv * pre[0, :, 512 + lo : 512 + hi]).astype(BF16)
        dpre[1, :, lo:hi] = (dq * pre[1, :, lo:hi]).astype(BF16)
        dpre[1, :, 512 + lo : 512 + hi] = (dk * pre[1, :, 512 + lo : 512 + hi]).astype(BF16)

    grad_chunks(x, y, 1 - c, nrm, dpre, mix, cot, gother)


def rest_body(
    nrm, dpre, mix, rstd, cot, w_in, w_out, a1, b1, a2, b2, a3, b3,
    gown, outgoing, dnorm, downed,
):
    x, y, c = lax.axis_index("x"), lax.axis_index("y"), lax.axis_index("c")
    proj, _ = weights_of(x, c, (w_in, w_out, (a1, a2, a3), (b1, b2, b3)))
    grad_chunks(x, y, c, nrm, dpre, mix, cot, gown)
    for k in range(4):
        total = None
        for is_own, h in ((True, c), (False, 1 - c)):
            part = dot(dpre[h], proj(k, is_own), NT)
            total = part if total is None else total + part
        dnorm[(x + 4 - k) % 4] = total.astype(BF16)

    def unnorm_rows(r, _):
        rows = pl.ds(pl.multiple_of(r * CHUNK, CHUNK), CHUNK)
        dn = jnp.concatenate([dnorm[j, rows, :] for j in range(4)], axis=1).astype(F32)
        hat = jnp.concatenate([nrm[j, rows, :] for j in range(4)], axis=1).astype(F32)
        m1 = jnp.sum(dn, axis=1, keepdims=True) * (1.0 / 1024)
        m2 = jnp.sum(dn * hat, axis=1, keepdims=True) * (1.0 / 1024)
        d = rstd[rows, :1] * (dn - m1 - hat * m2) + cot[rows, :].astype(F32)
        downed[rows, :] = d.astype(BF16)
        return 0

    lax.fori_loop(0, 256 // CHUNK, unnorm_rows, 0)
    t = iota((1024, 256), 1)
    wanted = (t & 63) * 16 + (t >> 6) * 4
    row = iota((1024, 256), 0)
    total = None
    for j in range(4):
        pick = (row == wanted + j).astype(F32).astype(BF16)
        part = dot(pick, downed[:, j * 256 : (j + 1) * 256])
        total = part if total is None else total + part
    outgoing[...] = total.astype(BF16)


def add_pair_body(own, other, *outs):
    for color in range(2):
        for s in range(4):
            both = own[color, s].astype(F32) + other[color, s].astype(F32)
            outs[color * 4 + s][...] = both.astype(BF16)


def add_four_body(a0, a1, a2, a3, b0, b1, b2, b3, *outs):
    for color, refs in enumerate(((a0, a1, a2, a3), (b0, b1, b2, b3))):
        for s in range(4):
            total = refs[0][s].astype(F32)
            for ref in refs[1:]:
                total = total + ref[s].astype(F32)
            outs[color * 4 + s][...] = total.astype(BF16)


def add_last_body(a0, a1, a2, a3, b0, b1, b2, b3, out):
    for color, refs in enumerate(((a0, a1, a2, a3), (b0, b1, b2, b3))):
        total = refs[0][...].astype(F32)
        for ref in refs[1:]:
            total = total + ref[...].astype(F32)
        total = total.astype(BF16)
        for j in range(4):
            out[color * 4 + j] = total[:, j * 128 : (j + 1) * 128]


def add_eight_body(parts, out):
    total = parts[0].astype(F32)
    for i in range(1, 8):
        total = total + parts[i].astype(F32)
    total = total.astype(BF16)
    for i in range(8):
        out[i] = total


def place_body(o0, o1, o2, o3, t0, t1, t2, t3, g_in, g_out, rows):
    y, c = lax.axis_index("y"), lax.axis_index("c")
    for refs, h in (((o0, o1, o2, o3), c), ((t0, t1, t2, t3), 1 - c)):
        for s in range(4):
            m = (y + 4 - s) % 4
            for j in range(8):
                rows[h, m, :, j * 128 : (j + 1) * 128] = refs[s][j]
    factor = 1.0 / 256.0
    for h in range(2):
        for m in range(3):
            g_in[80 * m : 80 * m + 80, h * 1024 : (h + 1) * 1024] = rows[h, m].astype(F32) * factor
        last = rows[h, 3].astype(F32) * factor
        g_in[240:, h * 1024 : (h + 1) * 1024] = last[:16]
        g_out[:64, h * 512 : (h + 1) * 512] = last[16:, :512]
        g_out[64:, h * 512 : (h + 1) * 512] = last[16:, 512:]


def shift(a, axis, n, s):
    return lax.ppermute(a, axis, [(i, (i + s) % n) for i in range(n)])


def on_device(x_rows, cotangent, w_in, w_out, hist_blocks, owner):
    cot = cotangent[0]
    outgoing, pack = call(
        prep_body,
        [((1024, 256), BF16), ((320, 1024), BF16)],
        (hist_blocks, owner, x_rows[0], w_in, w_out),
        "route_out",
    )
    own = [shift(pack, "x", 4, s) for s in (1, 2, 3)]
    other = [shift(a, "c", 2, 1) for a in own]
    arrived = lax.all_to_all(
        outgoing.reshape(64, 16, 256), DP, split_axis=0, concat_axis=0, tiled=True
    ).reshape(1024, 256)
    weights = (w_in, w_out, own[0], other[0], own[1], other[1], own[2], other[2])
    layer_out, gother, nrm, dpre, mix, rstd = call(
        layer_body,
        [
            ((256, 1024), BF16),
            ((2, 4, 4, 80, 512), BF16),
            ((4, 256, 256), BF16),
            ((2, 256, 1024), BF16),
            ((4, 256, 128), BF16),
            ((256, 128), F32),
        ],
        (hist_blocks, owner, arrived, cot) + weights,
        "layer",
        scratch=[
            ((256, 1024), F32),
            ((2, 256, 1024), F32),
            ((2, 256, 1024), BF16),
            ((256, 512), F32),
            ((256, 128), F32),
            ((4, 256, 256), BF16),
            ((4, 256, 256), F32),
            ((4, 256, 128), BF16),
            ((256, 512), BF16),
        ],
    )
    gfrom = shift(gother, "c", 2, 1)
    gown, backward = call(
        rest_body,
        [((2, 4, 4, 80, 512), BF16), ((1024, 256), BF16)],
        (nrm, dpre, mix, rstd, cot) + weights,
        "rest",
        scratch=[((4, 256, 256), BF16), ((256, 1024), BF16)],
    )
    big = call(add_pair_body, [((4, 80, 512), BF16)] * 8, (gown, gfrom), "add_pair")
    first = [big[0]] + [shift(big[s], "x", 4, s) for s in (1, 2, 3)]
    second = [big[4]] + [shift(big[4 + s], "y", 4, s) for s in (1, 2, 3)]
    returned = lax.all_to_all(
        backward.reshape(64, 16, 256), DP, split_axis=0, concat_axis=0, tiled=True
    ).reshape(1024, 256)
    (grad_rows,) = call(
        rows_back_body, [((128, 1024), BF16)], (hist_blocks, owner, returned), "route_back"
    )
    mid = call(add_four_body, [((80, 512), BF16)] * 8, (*first, *second), "add_four")
    first = [mid[0]] + [shift(mid[s], "y", 4, s) for s in (1, 2, 3)]
    second = [mid[4]] + [shift(mid[4 + s], "x", 4, s) for s in (1, 2, 3)]
    (columns,) = call(add_last_body, [((8, 80, 128), BF16)], (*first, *second), "add_last")
    parts = lax.all_to_all(columns, "z", split_axis=0, concat_axis=0, tiled=True)
    (summed,) = call(add_eight_body, [((8, 80, 128), BF16)], (parts,), "add_eight")
    mine = lax.all_to_all(summed, "z", split_axis=0, concat_axis=0, tiled=True)
    lines = [mine] + [shift(mine, "y", 4, s) for s in (1, 2, 3)]
    paired = [shift(a, "c", 2, 1) for a in lines]
    g_in, g_out = call(
        place_body,
        [((256, 2048), F32), ((128, 1024), F32)],
        (*lines, *paired),
        "place",
        scratch=[((2, 4, 80, 1024), BF16)],
    )
    return layer_out[None], grad_rows[None], g_in, g_out


def solution(mesh):
    fine = Mesh(mesh.devices.reshape(8, 4, 2, 4), ("z", "y", "c", "x"))
    placed = (
        P("x", DP, None),
        P("x", DP, None),
        P("x", None),
        P("x", None),
        P("x", None),
        P("x", None),
    )
    return jax.shard_map(
        on_device,
        mesh=fine,
        in_specs=placed,
        out_specs=(P("x", DP, None), P("x", DP, None), P("x", None), P("x", None)),
        check_vma=False,
    )
```

```python
import functools

import jax
import jax.numpy as jnp
from jax import lax
from jax.experimental import pallas as pl
from jax.experimental.pallas import tpu as pltpu
from jax.sharding import Mesh, PartitionSpec as P

F32 = jnp.float32
BF16 = jnp.bfloat16
EPS = 1e-06
HEAD = 128
DP = ("z", "y", "c")
NN = (((1,), (0,)), ((), ()))
NT = (((1,), (1,)), ((), ()))
TN = (((0,), (0,)), ((), ()))
VMEM_LIMIT = 24 * 1024 * 1024


def dot(a, b, dims=NN):
    return lax.dot_general(a, b, dims, preferred_element_type=F32)


def iota(shape, dim):
    return lax.broadcasted_iota(jnp.int32, shape, dim)


def call(body, outs, args, name, scratch=(), smem=0):
    return pl.pallas_call(
        body,
        out_shape=[jax.ShapeDtypeStruct(s, d) for s, d in outs],
        in_specs=[pl.BlockSpec(memory_space=pltpu.VMEM) for _ in args],
        out_specs=[pl.BlockSpec(memory_space=pltpu.VMEM) for _ in outs],
        scratch_shapes=[pltpu.VMEM(s, d) for s, d in scratch],
        compiler_params=pltpu.CompilerParams(vmem_limit_bytes=VMEM_LIMIT),
        name=name,
    )(*args)


def histories(blocks_ref, owners_ref):
    n_row = blocks_ref[...].astype(F32)
    o_row = owners_ref[...].astype(F32)
    count = n_row.shape[1]
    r, c = iota((count, count), 0), iota((count, count), 1)
    column = lambda cond, row: jnp.sum(jnp.where(cond, row, 0.0), axis=1, keepdims=True)
    n_col = column(r == c, n_row)
    o_col = column(r == c, o_row)
    start = column(c < r, n_row)
    same = o_col == o_row
    before_col = column((c < r) & same, n_row)
    before_row = jnp.sum(jnp.where((r < c) & same, n_col, 0.0), axis=0, keepdims=True)
    return n_row, o_row, n_col, o_col, start, before_col, before_row


def slots_of_rows(blocks_ref, owners_ref, count):
    _, _, n_col, o_col, start, before, _ = histories(blocks_ref, owners_ref)
    b = iota((n_col.shape[0], count), 1).astype(F32)
    inside = (start <= b) & (b < start + n_col)
    code = jnp.sum(jnp.where(inside, o_col * 4.0 + before - start, 0.0), axis=0, keepdims=True)
    return (code + b[:1]).astype(jnp.int32)


def pack_body(w_in_ref, w_out_ref, pack_ref):
    half = lax.axis_index("c")
    pack_ref[:256, :] = w_in_ref[:, pl.ds(pl.multiple_of(half * 1024, 1024), 1024)]
    wo = w_out_ref[:, pl.ds(pl.multiple_of(half * 512, 512), 512)]
    pack_ref[256:, :512] = wo[:64]
    pack_ref[256:, 512:] = wo[64:]


def rows_out_body(blocks_ref, owners_ref, x_ref, out_ref):
    code = slots_of_rows(blocks_ref, owners_ref, 128)
    row = iota((1024, 128), 0)
    total = None
    for j in range(4):
        pick = (row == code * 4 + j).astype(F32).astype(BF16)
        part = dot(pick, x_ref[:, j * 256 : (j + 1) * 256])
        total = part if total is None else total + part
    out_ref[...] = total.astype(BF16)


def rows_back(blocks_ref, owners_ref, returned_ref, out_ref):
    code = slots_of_rows(blocks_ref, owners_ref, 128)
    eye = iota((128, 128), 0) == iota((128, 128), 1)
    column = jnp.sum(jnp.where(eye, code.astype(F32), 0.0), axis=1, keepdims=True).astype(jnp.int32)
    lane = iota((128, 1024), 1)
    for j in range(4):
        pick = (lane == column * 4 + j).astype(F32).astype(BF16)
        out_ref[:, j * 256 : (j + 1) * 256] = dot(pick, returned_ref[...]).astype(BF16)


def weights_of(x, half, refs):
    w_in, w_out, own, other = refs
    other_half = 1 - half

    def proj(k, is_own):
        if k == 0:
            h = half if is_own else other_half
            return w_in[:, pl.ds(pl.multiple_of(h * 1024, 1024), 1024)]
        left, right, top, low = own if is_own else other
        if k == 2:
            return jnp.concatenate([top[...], low[:96, :]], axis=0)
        return (left if k == 1 else right)[:256, :]

    def back(k, is_own):
        if k == 0:
            h = half if is_own else other_half
            return w_out[:, pl.ds(pl.multiple_of(h * 512, 512), 512)]
        left, right, top, low = own if is_own else other
        part = low[96:, :] if k == 2 else (left if k == 1 else right)[256:, :]
        return jnp.concatenate([part[:, :512], part[:, 512:]], axis=0)

    return proj, back


def grad_chunks(x, y, half, nrm, dpre, mix, cot, put):
    right = cot[:, pl.ds(pl.multiple_of(half * 512, 512), 512)]
    for sx in range(4):
        block = (x + sx) % 4
        d_in = dot(nrm[block], dpre[half], TN).astype(BF16)
        d_out = dot(mix[block], right, TN).astype(BF16)
        tail = jnp.concatenate([d_out[:64], d_out[64:]], axis=1)
        for m in range(4):
            if m < 3:
                rows = d_in[80 * m : 80 * m + 80]
            else:
                rows = jnp.concatenate([d_in[240:], tail], axis=0)
            put(sx, (m + 4 - y) % 4, rows)


CHUNK = 32


def layer_body(
    blocks_ref, owners_ref, arrived, cot, w_in, w_out, a1, a2, a3, a4, b1, b2, b3, b4,
    layer_out, gother, nrm, dpre, mix, rstd,
    owned, pre, act, att, att_rstd, weights, dscore, dmixed, datt,
):
    x, y, c = lax.axis_index("x"), lax.axis_index("y"), lax.axis_index("c")
    me = (lax.axis_index("z") * 4 + y) * 2 + c
    proj, back = weights_of(x, c, (w_in, w_out, (a1, a2, a3, a4), (b1, b2, b3, b4)))
    halves = ((True, c), (False, 1 - c))

    t = iota((256, 1024), 0)
    wanted = (t & 63) * 16 + (t >> 6) * 4
    lane = iota((256, 1024), 1)
    for j in range(4):
        pick = (lane == wanted + j).astype(F32).astype(BF16)
        owned[:, j * 256 : (j + 1) * 256] = dot(pick, arrived[...])

    def norm_rows(r, _):
        rows = pl.ds(pl.multiple_of(r * CHUNK, CHUNK), CHUNK)
        v = owned[rows, :]
        cen = v - jnp.sum(v, axis=1, keepdims=True) * (1.0 / 1024)
        rs = lax.rsqrt(jnp.sum(cen * cen, axis=1, keepdims=True) * (1.0 / 1024) + EPS)
        n = (cen * rs).astype(BF16)
        for j in range(4):
            nrm[j, rows, :] = n[:, j * 256 : (j + 1) * 256]
        rstd[rows, :] = jnp.broadcast_to(rs, (CHUNK, 128))
        return 0

    lax.fori_loop(0, 256 // CHUNK, norm_rows, 0)

    for is_own, h in halves:
        total = None
        for k in range(4):
            part = dot(nrm[(x + 4 - k) % 4], proj(k, is_own))
            total = part if total is None else total + part
        pre[h] = total

    def activate(r, _):
        rows = pl.ds(pl.multiple_of(r * CHUNK, CHUNK), CHUNK)
        for h in range(2):
            v = pre[h, rows, :]
            sig = jax.nn.sigmoid(v)
            act[h, rows, :] = (v * sig).astype(BF16)
            pre[h, rows, :] = sig * (1.0 + v * (1.0 - sig))
        return 0

    lax.fori_loop(0, 256 // CHUNK, activate, 0)

    n_row, o_row, n_col, o_col, _, before_col, before_row = histories(blocks_ref, owners_ref)
    mine = me.astype(F32)
    label = 1.0 + iota((64, 256), 0).astype(F32)
    at = iota((64, 256), 1).astype(F32)
    inside = (o_col == mine) & (at >= before_col * 64.0) & (at < (before_col + n_col) * 64.0)
    seg_row = jnp.sum(jnp.where(inside, label, 0.0), axis=0, keepdims=True)
    label = 1.0 + iota((256, 64), 1).astype(F32)
    at = iota((256, 64), 0).astype(F32)
    inside = (o_row == mine) & (at >= before_row * 64.0) & (at < (before_row + n_row) * 64.0)
    seg_col = jnp.sum(jnp.where(inside, label, 0.0), axis=1, keepdims=True)
    visible = (seg_row == seg_col) & (iota((256, 256), 1) <= iota((256, 256), 0)) & (seg_col > 0.0)
    mask = jnp.where(visible, 1.0 / 256.0, 0.0)

    scale = HEAD ** (-0.5)
    for h in range(4):
        lo, hi = h * HEAD, (h + 1) * HEAD
        s = dot(act[1, :, lo:hi], act[1, :, 512 + lo : 512 + hi], NT) * scale
        sig = jax.nn.sigmoid(s)
        w = (s * sig * mask).astype(BF16)
        weights[h] = w
        dscore[h] = mask * (sig * (1.0 + s * (1.0 - sig))) * scale
        att[:, lo:hi] = dot(w, act[0, :, 512 + lo : 512 + hi])

    def mix_rows(r, _):
        rows = pl.ds(pl.multiple_of(r * CHUNK, CHUNK), CHUNK)
        v = att[rows, :]
        cen = v - jnp.sum(v, axis=1, keepdims=True) * (1.0 / 512)
        rs = lax.rsqrt(jnp.sum(cen * cen, axis=1, keepdims=True) * (1.0 / 512) + EPS)
        hat = cen * rs
        mixed = (act[0, rows, :512].astype(F32) * hat).astype(BF16)
        for h in range(4):
            mix[h, rows, :] = mixed[:, h * HEAD : (h + 1) * HEAD]
        att[rows, :] = hat
        att_rstd[rows, :] = jnp.broadcast_to(rs, (CHUNK, 128))
        return 0

    lax.fori_loop(0, 256 // CHUNK, mix_rows, 0)

    for is_own, h in halves:
        columns = pl.ds(pl.multiple_of(h * 512, 512), 512)
        total = owned[:, columns]
        for k in range(4):
            total = total + dot(mix[(x + 4 - k) % 4], back(k, is_own))
        layer_out[:, columns] = total.astype(BF16)

    for k in range(4):
        total = None
        for is_own, h in halves:
            columns = pl.ds(pl.multiple_of(h * 512, 512), 512)
            part = dot(cot[:, columns], back(k, is_own), NT)
            total = part if total is None else total + part
        dmixed[(x + 4 - k) % 4] = total.astype(BF16)

    def unmix_rows(r, _):
        rows = pl.ds(pl.multiple_of(r * CHUNK, CHUNK), CHUNK)
        dm = jnp.concatenate([dmixed[h, rows, :] for h in range(4)], axis=1).astype(F32)
        hat = att[rows, :]
        du = (dm * hat).astype(BF16).astype(F32)
        dpre[0, rows, :512] = (du * pre[0, rows, :512]).astype(BF16)
        dh = dm * act[0, rows, :512].astype(F32)
        m1 = jnp.sum(dh, axis=1, keepdims=True) * (1.0 / 512)
        m2 = jnp.sum(dh * hat, axis=1, keepdims=True) * (1.0 / 512)
        datt[rows, :] = (att_rstd[rows, :1] * (dh - m1 - hat * m2)).astype(BF16)
        return 0

    lax.fori_loop(0, 256 // CHUNK, unmix_rows, 0)

    for h in range(4):
        lo, hi = h * HEAD, (h + 1) * HEAD
        d_h = datt[:, lo:hi]
        dw = dot(d_h, act[0, :, 512 + lo : 512 + hi], NT).astype(BF16).astype(F32)
        ds = (dw * dscore[h]).astype(BF16)
        dv = dot(weights[h], d_h, TN).astype(BF16).astype(F32)
        dq = dot(ds, act[1, :, 512 + lo : 512 + hi]).astype(BF16).astype(F32)
        dk = dot(ds, act[1, :, lo:hi], TN).astype(BF16).astype(F32)
        dpre[0, :, 512 + lo : 512 + hi] = (dv * pre[0, :, 512 + lo : 512 + hi]).astype(BF16)
        dpre[1, :, lo:hi] = (dq * pre[1, :, lo:hi]).astype(BF16)
        dpre[1, :, 512 + lo : 512 + hi] = (dk * pre[1, :, 512 + lo : 512 + hi]).astype(BF16)

    def put(sx, sy, rows):
        gother[0, sx, sy] = rows[:, :512]
        gother[1, sy, sx] = rows[:, 512:]

    grad_chunks(x, y, 1 - c, nrm, dpre, mix, cot, put)


def rest_body(
    nrm, dpre, rstd, cot, w_in, w_out, a1, a2, a3, a4, b1, b2, b3, b4,
    downed, dnorm,
):
    x, c = lax.axis_index("x"), lax.axis_index("c")
    proj, _ = weights_of(x, c, (w_in, w_out, (a1, a2, a3, a4), (b1, b2, b3, b4)))
    for k in range(4):
        total = None
        for is_own, h in ((True, c), (False, 1 - c)):
            part = dot(dpre[h], proj(k, is_own), NT)
            total = part if total is None else total + part
        dnorm[(x + 4 - k) % 4] = total.astype(BF16)

    def unnorm_rows(r, _):
        rows = pl.ds(pl.multiple_of(r * CHUNK, CHUNK), CHUNK)
        dn = jnp.concatenate([dnorm[j, rows, :] for j in range(4)], axis=1).astype(F32)
        hat = jnp.concatenate([nrm[j, rows, :] for j in range(4)], axis=1).astype(F32)
        m1 = jnp.sum(dn, axis=1, keepdims=True) * (1.0 / 1024)
        m2 = jnp.sum(dn * hat, axis=1, keepdims=True) * (1.0 / 1024)
        d = rstd[rows, :1] * (dn - m1 - hat * m2) + cot[rows, :].astype(F32)
        downed[rows, :] = d.astype(BF16)
        return 0

    lax.fori_loop(0, 256 // CHUNK, unnorm_rows, 0)

def sum_pair_body(nrm, dpre, mix, cot, downed, gfrom, *refs):
    outs, outgoing, held = refs[:8], refs[8], refs[9]
    x, y, c = lax.axis_index("x"), lax.axis_index("y"), lax.axis_index("c")

    def put(sx, sy, rows):
        rows = rows.astype(F32)
        outs[sx][sy] = (rows[:, :512] + gfrom[0, sx, sy].astype(F32)).astype(BF16)
        held[sy, sx] = (rows[:, 512:] + gfrom[1, sy, sx].astype(F32)).astype(BF16)

    grad_chunks(x, y, c, nrm, dpre, mix, cot, put)
    for sy in range(4):
        outs[4 + sy][...] = held[sy]
    t = iota((1024, 256), 1)
    wanted = (t & 63) * 16 + (t >> 6) * 4
    row = iota((1024, 256), 0)
    total = None
    for j in range(4):
        pick = (row == wanted + j).astype(F32).astype(BF16)
        part = dot(pick, downed[:, j * 256 : (j + 1) * 256])
        total = part if total is None else total + part
    outgoing[...] = total.astype(BF16)


def add_four_body(a0, a1, a2, a3, b0, b1, b2, b3, blocks, owners, returned, rows, *outs):
    rows_back(blocks, owners, returned, rows)
    for color, refs in enumerate(((a0, a1, a2, a3), (b0, b1, b2, b3))):
        for s in range(4):
            total = refs[0][s].astype(F32)
            for ref in refs[1:]:
                total = total + ref[s].astype(F32)
            outs[color * 4 + s][...] = total.astype(BF16)


def add_last_body(a0, a1, a2, a3, b0, b1, b2, b3, out):
    for color, refs in enumerate(((a0, a1, a2, a3), (b0, b1, b2, b3))):
        total = refs[0][...].astype(F32)
        for ref in refs[1:]:
            total = total + ref[...].astype(F32)
        total = total.astype(BF16)
        for j in range(4):
            out[color * 4 + j] = total[:, j * 128 : (j + 1) * 128]


def add_eight_body(parts, out):
    total = parts[0].astype(F32)
    for i in range(1, 8):
        total = total + parts[i].astype(F32)
    total = total.astype(BF16)
    for i in range(8):
        out[i] = total


def place_body(o0, o1, o2, o3, t0, t1, t2, t3, g_in, g_out, rows):
    y, c = lax.axis_index("y"), lax.axis_index("c")
    for refs, h in (((o0, o1, o2, o3), c), ((t0, t1, t2, t3), 1 - c)):
        for s in range(4):
            m = (y + 4 - s) % 4
            for j in range(8):
                rows[h, m, :, j * 128 : (j + 1) * 128] = refs[s][j]
    factor = 1.0 / 256.0
    for h in range(2):
        for m in range(3):
            g_in[80 * m : 80 * m + 80, h * 1024 : (h + 1) * 1024] = rows[h, m].astype(F32) * factor
        last = rows[h, 3].astype(F32) * factor
        g_in[240:, h * 1024 : (h + 1) * 1024] = last[:16]
        g_out[:64, h * 512 : (h + 1) * 512] = last[16:, :512]
        g_out[64:, h * 512 : (h + 1) * 512] = last[16:, 512:]


def shift(a, axis, n, s):
    return lax.ppermute(a, axis, [(i, (i + s) % n) for i in range(n)])


def on_device(x_rows, cotangent, w_in, w_out, hist_blocks, owner):
    cot = cotangent[0]
    (pack,) = call(pack_body, [((320, 1024), BF16)], (w_in, w_out), "pack")
    left, right = shift(pack, "x", 4, 1), shift(pack, "x", 4, 3)
    (outgoing,) = call(
        rows_out_body, [((1024, 256), BF16)], (hist_blocks, owner, x_rows[0]), "rows_out"
    )
    arrived = lax.all_to_all(
        outgoing.reshape(64, 16, 256), DP, split_axis=0, concat_axis=0, tiled=True
    ).reshape(1024, 256)
    own = [left, right, shift(left[:160], "x", 4, 1), shift(right[160:], "x", 4, 3)]
    weights = (w_in, w_out, *own, *[shift(a, "c", 2, 1) for a in own])
    layer_out, gother, nrm, dpre, mix, rstd = call(
        layer_body,
        [
            ((256, 1024), BF16),
            ((2, 4, 4, 80, 512), BF16),
            ((4, 256, 256), BF16),
            ((2, 256, 1024), BF16),
            ((4, 256, 128), BF16),
            ((256, 128), F32),
        ],
        (hist_blocks, owner, arrived, cot) + weights,
        "layer",
        scratch=[
            ((256, 1024), F32),
            ((2, 256, 1024), F32),
            ((2, 256, 1024), BF16),
            ((256, 512), F32),
            ((256, 128), F32),
            ((4, 256, 256), BF16),
            ((4, 256, 256), F32),
            ((4, 256, 128), BF16),
            ((256, 512), BF16),
        ],
    )
    gfrom = shift(gother, "c", 2, 1)
    (downed,) = call(
        rest_body,
        [((256, 1024), BF16)],
        (nrm, dpre, rstd, cot) + weights,
        "rest",
        scratch=[((4, 256, 256), BF16)],
    )
    *big, backward = call(
        sum_pair_body,
        [((4, 80, 512), BF16)] * 8 + [((1024, 256), BF16)],
        (nrm, dpre, mix, cot, downed, gfrom),
        "sum_pair",
        scratch=[((4, 4, 80, 512), BF16)],
    )
    first = [big[0]] + [shift(big[s], "x", 4, s) for s in (1, 2, 3)]
    second = [big[4]] + [shift(big[4 + s], "y", 4, s) for s in (1, 2, 3)]
    returned = lax.all_to_all(
        backward.reshape(64, 16, 256), DP, split_axis=0, concat_axis=0, tiled=True
    ).reshape(1024, 256)
    grad_rows, *mid = call(
        add_four_body,
        [((128, 1024), BF16)] + [((80, 512), BF16)] * 8,
        (*first, *second, hist_blocks, owner, returned),
        "add_four",
    )
    first = [mid[0]] + [shift(mid[s], "y", 4, s) for s in (1, 2, 3)]
    second = [mid[4]] + [shift(mid[4 + s], "x", 4, s) for s in (1, 2, 3)]
    (columns,) = call(add_last_body, [((8, 80, 128), BF16)], (*first, *second), "add_last")
    parts = lax.all_to_all(columns, "z", split_axis=0, concat_axis=0, tiled=True)
    (summed,) = call(add_eight_body, [((8, 80, 128), BF16)], (parts,), "add_eight")
    mine = lax.all_to_all(summed, "z", split_axis=0, concat_axis=0, tiled=True)
    lines = [mine] + [shift(mine, "y", 4, s) for s in (1, 2, 3)]
    paired = [shift(a, "c", 2, 1) for a in lines]
    g_in, g_out = call(
        place_body,
        [((256, 2048), F32), ((128, 1024), F32)],
        (*lines, *paired),
        "place",
        scratch=[((2, 4, 80, 1024), BF16)],
    )
    return layer_out[None], grad_rows[None], g_in, g_out


def solution(mesh):
    fine = Mesh(mesh.devices.reshape(8, 4, 2, 4), ("z", "y", "c", "x"))
    placed = (
        P("x", DP, None),
        P("x", DP, None),
        P("x", None),
        P("x", None),
        P("x", None),
        P("x", None),
    )
    return jax.shard_map(
        on_device,
        mesh=fine,
        in_specs=placed,
        out_specs=(P("x", DP, None), P("x", DP, None), P("x", None), P("x", None)),
        check_vma=False,
    )
```

```python
import functools

import jax
import jax.numpy as jnp
from jax import lax
from jax.experimental import pallas as pl
from jax.experimental.pallas import tpu as pltpu
from jax.sharding import Mesh, PartitionSpec as P

F32 = jnp.float32
BF16 = jnp.bfloat16
EPS = 1e-06
HEAD = 128
DP = ("z", "y", "c")
NN = (((1,), (0,)), ((), ()))
NT = (((1,), (1,)), ((), ()))
TN = (((0,), (0,)), ((), ()))
VMEM_LIMIT = 24 * 1024 * 1024


def dot(a, b, dims=NN):
    return lax.dot_general(a, b, dims, preferred_element_type=F32)


def iota(shape, dim):
    return lax.broadcasted_iota(jnp.int32, shape, dim)


def call(body, outs, args, name, scratch=(), smem=0):
    return pl.pallas_call(
        body,
        out_shape=[jax.ShapeDtypeStruct(s, d) for s, d in outs],
        in_specs=[pl.BlockSpec(memory_space=pltpu.VMEM) for _ in args],
        out_specs=[pl.BlockSpec(memory_space=pltpu.VMEM) for _ in outs],
        scratch_shapes=[pltpu.VMEM(s, d) for s, d in scratch],
        compiler_params=pltpu.CompilerParams(vmem_limit_bytes=VMEM_LIMIT),
        name=name,
    )(*args)


def histories(blocks_ref, owners_ref):
    n_row = blocks_ref[...].astype(F32)
    o_row = owners_ref[...].astype(F32)
    count = n_row.shape[1]
    r, c = iota((count, count), 0), iota((count, count), 1)
    column = lambda cond, row: jnp.sum(jnp.where(cond, row, 0.0), axis=1, keepdims=True)
    n_col = column(r == c, n_row)
    o_col = column(r == c, o_row)
    start = column(c < r, n_row)
    same = o_col == o_row
    before_col = column((c < r) & same, n_row)
    before_row = jnp.sum(jnp.where((r < c) & same, n_col, 0.0), axis=0, keepdims=True)
    return n_row, o_row, n_col, o_col, start, before_col, before_row


def slots_of_rows(blocks_ref, owners_ref, count):
    _, _, n_col, o_col, start, before, _ = histories(blocks_ref, owners_ref)
    b = iota((n_col.shape[0], count), 1).astype(F32)
    inside = (start <= b) & (b < start + n_col)
    code = jnp.sum(jnp.where(inside, o_col * 4.0 + before - start, 0.0), axis=0, keepdims=True)
    return (code + b[:1]).astype(jnp.int32)


def entry_body(blocks_hbm, owners_hbm, x_hbm, w_in, w_out, out_ref, pack, blocks, owners, rows, sems):
    half = lax.axis_index("c")
    wide = pl.ds(pl.multiple_of(half * 1024, 1024), 1024)
    left = pl.ds(pl.multiple_of(half * 1024 // 2, 512), 512)
    copies = [
        pltpu.make_async_copy(a, b, sems.at[i])
        for i, (a, b) in enumerate(
            (
                (blocks_hbm, blocks),
                (owners_hbm, owners),
                (x_hbm, rows),
                (w_in.at[:, wide], pack.at[pl.ds(0, 256), :]),
                (w_out.at[pl.ds(0, 64), left], pack.at[pl.ds(256, 64), pl.ds(0, 512)]),
                (w_out.at[pl.ds(64, 64), left], pack.at[pl.ds(256, 64), pl.ds(512, 512)]),
            )
        )
    ]
    for copy in copies:
        copy.start()
    for copy in copies[:3]:
        copy.wait()
    code = slots_of_rows(blocks, owners, 128)
    row = iota((1024, 128), 0)
    total = None
    for j in range(4):
        pick = (row == code * 4 + j).astype(F32).astype(BF16)
        part = dot(pick, rows[:, j * 256 : (j + 1) * 256])
        total = part if total is None else total + part
    out_ref[...] = total.astype(BF16)
    for copy in copies[3:]:
        copy.wait()


def rows_back(blocks_ref, owners_ref, returned_ref, out_ref):
    code = slots_of_rows(blocks_ref, owners_ref, 128)
    eye = iota((128, 128), 0) == iota((128, 128), 1)
    column = jnp.sum(jnp.where(eye, code.astype(F32), 0.0), axis=1, keepdims=True).astype(jnp.int32)
    lane = iota((128, 1024), 1)
    for j in range(4):
        pick = (lane == column * 4 + j).astype(F32).astype(BF16)
        out_ref[:, j * 256 : (j + 1) * 256] = dot(pick, returned_ref[...]).astype(BF16)


def weights_of(x, half, refs):
    w_in, w_out, own, other = refs
    other_half = 1 - half

    def proj(k, is_own):
        if k == 0:
            h = half if is_own else other_half
            return w_in[:, pl.ds(pl.multiple_of(h * 1024, 1024), 1024)]
        left, right, top, low = own if is_own else other
        if k == 2:
            return jnp.concatenate([top[...], low[:96, :]], axis=0)
        return (left if k == 1 else right)[:256, :]

    def back(k, is_own):
        if k == 0:
            h = half if is_own else other_half
            return w_out[:, pl.ds(pl.multiple_of(h * 512, 512), 512)]
        left, right, top, low = own if is_own else other
        part = low[96:, :] if k == 2 else (left if k == 1 else right)[256:, :]
        return jnp.concatenate([part[:, :512], part[:, 512:]], axis=0)

    return proj, back


def grad_chunks(x, y, half, nrm, dpre, mix, cot, put):
    right = cot[:, pl.ds(pl.multiple_of(half * 512, 512), 512)]
    for sx in range(4):
        block = (x + sx) % 4
        d_in = dot(nrm[block], dpre[half], TN).astype(BF16)
        d_out = dot(mix[block], right, TN).astype(BF16)
        tail = jnp.concatenate([d_out[:64], d_out[64:]], axis=1)
        for m in range(4):
            if m < 3:
                rows = d_in[80 * m : 80 * m + 80]
            else:
                rows = jnp.concatenate([d_in[240:], tail], axis=0)
            put(sx, (m + 4 - y) % 4, rows)


def order_of(half, sx, sy):
    return jnp.where(half == 0, sx, sy), jnp.where(half == 0, sy, sx)


CHUNK = 32


def layer_body(
    blocks_ref, owners_ref, arrived, cot, w_in, w_out, a1, a2, a3, a4, b1, b2, b3, b4,
    layer_out, gother, nrm, dpre, mix, rstd,
    owned, pre, act, att, att_rstd, weights, dscore, dmixed, datt,
):
    x, y, c = lax.axis_index("x"), lax.axis_index("y"), lax.axis_index("c")
    me = (lax.axis_index("z") * 4 + y) * 2 + c
    proj, back = weights_of(x, c, (w_in, w_out, (a1, a2, a3, a4), (b1, b2, b3, b4)))
    halves = ((True, c), (False, 1 - c))

    t = iota((256, 1024), 0)
    wanted = (t & 63) * 16 + (t >> 6) * 4
    lane = iota((256, 1024), 1)
    for j in range(4):
        pick = (lane == wanted + j).astype(F32).astype(BF16)
        owned[:, j * 256 : (j + 1) * 256] = dot(pick, arrived[...])

    def norm_rows(r, _):
        rows = pl.ds(pl.multiple_of(r * CHUNK, CHUNK), CHUNK)
        v = owned[rows, :]
        cen = v - jnp.sum(v, axis=1, keepdims=True) * (1.0 / 1024)
        rs = lax.rsqrt(jnp.sum(cen * cen, axis=1, keepdims=True) * (1.0 / 1024) + EPS)
        n = (cen * rs).astype(BF16)
        for j in range(4):
            nrm[j, rows, :] = n[:, j * 256 : (j + 1) * 256]
        rstd[rows, :] = jnp.broadcast_to(rs, (CHUNK, 128))
        return 0

    lax.fori_loop(0, 256 // CHUNK, norm_rows, 0)

    for is_own, h in halves:
        total = None
        for k in range(4):
            part = dot(nrm[(x + 4 - k) % 4], proj(k, is_own))
            total = part if total is None else total + part
        pre[h] = total

    def activate(r, _):
        rows = pl.ds(pl.multiple_of(r * CHUNK, CHUNK), CHUNK)
        for h in range(2):
            v = pre[h, rows, :]
            sig = jax.nn.sigmoid(v)
            act[h, rows, :] = (v * sig).astype(BF16)
            pre[h, rows, :] = sig * (1.0 + v * (1.0 - sig))
        return 0

    lax.fori_loop(0, 256 // CHUNK, activate, 0)

    n_row, o_row, n_col, o_col, _, before_col, before_row = histories(blocks_ref, owners_ref)
    mine = me.astype(F32)
    label = 1.0 + iota((64, 256), 0).astype(F32)
    at = iota((64, 256), 1).astype(F32)
    inside = (o_col == mine) & (at >= before_col * 64.0) & (at < (before_col + n_col) * 64.0)
    seg_row = jnp.sum(jnp.where(inside, label, 0.0), axis=0, keepdims=True)
    label = 1.0 + iota((256, 64), 1).astype(F32)
    at = iota((256, 64), 0).astype(F32)
    inside = (o_row == mine) & (at >= before_row * 64.0) & (at < (before_row + n_row) * 64.0)
    seg_col = jnp.sum(jnp.where(inside, label, 0.0), axis=1, keepdims=True)
    visible = (seg_row == seg_col) & (iota((256, 256), 1) <= iota((256, 256), 0)) & (seg_col > 0.0)
    mask = jnp.where(visible, 1.0 / 256.0, 0.0)

    scale = HEAD ** (-0.5)
    for h in range(4):
        lo, hi = h * HEAD, (h + 1) * HEAD
        s = dot(act[1, :, lo:hi], act[1, :, 512 + lo : 512 + hi], NT) * scale
        sig = jax.nn.sigmoid(s)
        w = (s * sig * mask).astype(BF16)
        weights[h] = w
        dscore[h] = mask * (sig * (1.0 + s * (1.0 - sig))) * scale
        att[:, lo:hi] = dot(w, act[0, :, 512 + lo : 512 + hi])

    def mix_rows(r, _):
        rows = pl.ds(pl.multiple_of(r * CHUNK, CHUNK), CHUNK)
        v = att[rows, :]
        cen = v - jnp.sum(v, axis=1, keepdims=True) * (1.0 / 512)
        rs = lax.rsqrt(jnp.sum(cen * cen, axis=1, keepdims=True) * (1.0 / 512) + EPS)
        hat = cen * rs
        mixed = (act[0, rows, :512].astype(F32) * hat).astype(BF16)
        for h in range(4):
            mix[h, rows, :] = mixed[:, h * HEAD : (h + 1) * HEAD]
        att[rows, :] = hat
        att_rstd[rows, :] = jnp.broadcast_to(rs, (CHUNK, 128))
        return 0

    lax.fori_loop(0, 256 // CHUNK, mix_rows, 0)

    for is_own, h in halves:
        columns = pl.ds(pl.multiple_of(h * 512, 512), 512)
        total = owned[:, columns]
        for k in range(4):
            total = total + dot(mix[(x + 4 - k) % 4], back(k, is_own))
        layer_out[:, columns] = total.astype(BF16)

    for k in range(4):
        total = None
        for is_own, h in halves:
            columns = pl.ds(pl.multiple_of(h * 512, 512), 512)
            part = dot(cot[:, columns], back(k, is_own), NT)
            total = part if total is None else total + part
        dmixed[(x + 4 - k) % 4] = total.astype(BF16)

    def unmix_rows(r, _):
        rows = pl.ds(pl.multiple_of(r * CHUNK, CHUNK), CHUNK)
        dm = jnp.concatenate([dmixed[h, rows, :] for h in range(4)], axis=1).astype(F32)
        hat = att[rows, :]
        du = (dm * hat).astype(BF16).astype(F32)
        dpre[0, rows, :512] = (du * pre[0, rows, :512]).astype(BF16)
        dh = dm * act[0, rows, :512].astype(F32)
        m1 = jnp.sum(dh, axis=1, keepdims=True) * (1.0 / 512)
        m2 = jnp.sum(dh * hat, axis=1, keepdims=True) * (1.0 / 512)
        datt[rows, :] = (att_rstd[rows, :1] * (dh - m1 - hat * m2)).astype(BF16)
        return 0

    lax.fori_loop(0, 256 // CHUNK, unmix_rows, 0)

    for h in range(4):
        lo, hi = h * HEAD, (h + 1) * HEAD
        d_h = datt[:, lo:hi]
        dw = dot(d_h, act[0, :, 512 + lo : 512 + hi], NT).astype(BF16).astype(F32)
        ds = (dw * dscore[h]).astype(BF16)
        dv = dot(weights[h], d_h, TN).astype(BF16).astype(F32)
        dq = dot(ds, act[1, :, 512 + lo : 512 + hi]).astype(BF16).astype(F32)
        dk = dot(ds, act[1, :, lo:hi], TN).astype(BF16).astype(F32)
        dpre[0, :, 512 + lo : 512 + hi] = (dv * pre[0, :, 512 + lo : 512 + hi]).astype(BF16)
        dpre[1, :, lo:hi] = (dq * pre[1, :, lo:hi]).astype(BF16)
        dpre[1, :, 512 + lo : 512 + hi] = (dk * pre[1, :, 512 + lo : 512 + hi]).astype(BF16)

    def put(sx, sy, rows):
        first, second = order_of(1 - c, sx, sy)
        gother[first, second] = rows

    grad_chunks(x, y, 1 - c, nrm, dpre, mix, cot, put)


def rest_body(
    nrm, dpre, rstd, cot, w_in, w_out, a1, a2, a3, a4, b1, b2, b3, b4,
    outgoing, dnorm, downed,
):
    x, c = lax.axis_index("x"), lax.axis_index("c")
    proj, _ = weights_of(x, c, (w_in, w_out, (a1, a2, a3, a4), (b1, b2, b3, b4)))
    for k in range(4):
        total = None
        for is_own, h in ((True, c), (False, 1 - c)):
            part = dot(dpre[h], proj(k, is_own), NT)
            total = part if total is None else total + part
        dnorm[(x + 4 - k) % 4] = total.astype(BF16)

    def unnorm_rows(r, _):
        rows = pl.ds(pl.multiple_of(r * CHUNK, CHUNK), CHUNK)
        dn = jnp.concatenate([dnorm[j, rows, :] for j in range(4)], axis=1).astype(F32)
        hat = jnp.concatenate([nrm[j, rows, :] for j in range(4)], axis=1).astype(F32)
        m1 = jnp.sum(dn, axis=1, keepdims=True) * (1.0 / 1024)
        m2 = jnp.sum(dn * hat, axis=1, keepdims=True) * (1.0 / 1024)
        d = rstd[rows, :1] * (dn - m1 - hat * m2) + cot[rows, :].astype(F32)
        downed[rows, :] = d.astype(BF16)
        return 0

    lax.fori_loop(0, 256 // CHUNK, unnorm_rows, 0)
    t = iota((1024, 256), 1)
    wanted = (t & 63) * 16 + (t >> 6) * 4
    row = iota((1024, 256), 0)
    total = None
    for j in range(4):
        pick = (row == wanted + j).astype(F32).astype(BF16)
        part = dot(pick, downed[:, j * 256 : (j + 1) * 256])
        total = part if total is None else total + part
    outgoing[...] = total.astype(BF16)

def sum_pair_body(nrm, dpre, mix, cot, gfrom, backward, ahead, behind, kept, held):
    x, y, c = lax.axis_index("x"), lax.axis_index("y"), lax.axis_index("c")

    def put(sx, sy, rows):
        first, second = order_of(c, sx, sy)
        held[first, second] = (rows.astype(F32) + gfrom[first, second].astype(F32)).astype(BF16)

    grad_chunks(x, y, c, nrm, dpre, mix, cot, put)
    ahead[0] = held[2, :2]
    ahead[1] = held[1, 2:]
    behind[0] = held[2, 2:]
    behind[1] = held[3, :2]
    kept[:4] = held[0]
    kept[4:6] = held[1, :2]
    kept[6:] = held[3, 2:]


def add_relayed_body(kept, ahead, behind, forth, back):
    forth[...] = (kept[4:6].astype(F32) + ahead[0].astype(F32)).astype(BF16)
    back[...] = (kept[6:].astype(F32) + behind[0].astype(F32)).astype(BF16)


def add_four_body(kept, ahead, behind, forth, back, *outs):
    for s in range(4):
        if s < 2:
            total = kept[s].astype(F32) + behind[1, s].astype(F32) + forth[s].astype(F32)
        else:
            total = kept[s].astype(F32) + ahead[1, s - 2].astype(F32) + back[s - 2].astype(F32)
        outs[s][...] = total.astype(BF16)


def add_last_body(a0, a1, a2, a3, out):
    total = a0[...].astype(F32) + a1[...].astype(F32) + a2[...].astype(F32) + a3[...].astype(F32)
    total = total.astype(BF16)
    for j in range(8):
        out[j] = total[:, j * 128 : (j + 1) * 128]


def add_eight_body(parts, out):
    total = parts[0].astype(F32)
    for i in range(1, 8):
        total = total + parts[i].astype(F32)
    total = total.astype(BF16)
    for i in range(8):
        out[i] = total


def place_body(o0, o1, o2, o3, t0, t1, t2, t3, g_in, g_out, rows):
    y, c = lax.axis_index("y"), lax.axis_index("c")
    for refs, h in (((o0, o1, o2, o3), c), ((t0, t1, t2, t3), 1 - c)):
        for s in range(4):
            m = (y + 4 - s) % 4
            for j in range(8):
                rows[h, m, :, j * 128 : (j + 1) * 128] = refs[s][j]
    factor = 1.0 / 256.0
    for h in range(2):
        for m in range(3):
            g_in[80 * m : 80 * m + 80, h * 1024 : (h + 1) * 1024] = rows[h, m].astype(F32) * factor
        last = rows[h, 3].astype(F32) * factor
        g_in[240:, h * 1024 : (h + 1) * 1024] = last[:16]
        g_out[:64, h * 512 : (h + 1) * 512] = last[16:, :512]
        g_out[64:, h * 512 : (h + 1) * 512] = last[16:, 512:]


def shift(a, axis, n, s):
    return lax.ppermute(a, axis, [(i, (i + s) % n) for i in range(n)])


def crossed(a, s, first):
    pairs = []
    for z in range(8):
        for y in range(4):
            for c in range(2):
                for x in range(4):
                    over_x = (c == 0) == first
                    ty, tx = (y, (x + s) % 4) if over_x else ((y + s) % 4, x)
                    at = lambda v, w: ((z * 4 + v) * 2 + c) * 4 + w
                    pairs.append((at(y, x), at(ty, tx)))
    return lax.ppermute(a, ("z", "y", "c", "x"), pairs)


def on_device(x_rows, cotangent, w_in, w_out, hist_blocks, owner):
    cot = cotangent[0]
    hbm = pl.BlockSpec(memory_space=pltpu.HBM)
    outgoing, pack = pl.pallas_call(
        entry_body,
        out_shape=[
            jax.ShapeDtypeStruct((1024, 256), BF16),
            jax.ShapeDtypeStruct((320, 1024), BF16),
        ],
        in_specs=[hbm] * 5,
        out_specs=[pl.BlockSpec(memory_space=pltpu.VMEM)] * 2,
        scratch_shapes=[
            pltpu.VMEM((1, 64), jnp.int32),
            pltpu.VMEM((1, 64), jnp.int32),
            pltpu.VMEM((128, 1024), BF16),
            pltpu.SemaphoreType.DMA((6,)),
        ],
        compiler_params=pltpu.CompilerParams(vmem_limit_bytes=60 * 1024 * 1024),
        name="entry",
    )(hist_blocks, owner, x_rows[0], w_in, w_out)
    left, right = shift(pack, "x", 4, 1), shift(pack, "x", 4, 3)
    arrived = lax.all_to_all(
        outgoing.reshape(64, 16, 256), DP, split_axis=0, concat_axis=0, tiled=True
    ).reshape(1024, 256)
    own = [left, right, shift(left[:160], "x", 4, 1), shift(right[160:], "x", 4, 3)]
    weights = (w_in, w_out, *own, *[shift(a, "c", 2, 1) for a in own])
    layer_out, gother, nrm, dpre, mix, rstd = call(
        layer_body,
        [
            ((256, 1024), BF16),
            ((4, 4, 80, 1024), BF16),
            ((4, 256, 256), BF16),
            ((2, 256, 1024), BF16),
            ((4, 256, 128), BF16),
            ((256, 128), F32),
        ],
        (hist_blocks, owner, arrived, cot) + weights,
        "layer",
        scratch=[
            ((256, 1024), F32),
            ((2, 256, 1024), F32),
            ((2, 256, 1024), BF16),
            ((256, 512), F32),
            ((256, 128), F32),
            ((4, 256, 256), BF16),
            ((4, 256, 256), F32),
            ((4, 256, 128), BF16),
            ((256, 512), BF16),
        ],
    )
    gfrom = shift(gother, "c", 2, 1)
    (backward,) = call(
        rest_body,
        [((1024, 256), BF16)],
        (nrm, dpre, rstd, cot) + weights,
        "rest",
        scratch=[((4, 256, 256), BF16), ((256, 1024), BF16)],
    )
    ahead, behind, kept = call(
        sum_pair_body,
        [((2, 2, 80, 1024), BF16), ((2, 2, 80, 1024), BF16), ((8, 80, 1024), BF16)],
        (nrm, dpre, mix, cot, gfrom, backward),
        "sum_pair",
        scratch=[((4, 4, 80, 1024), BF16)],
    )
    backward, kept = lax.optimization_barrier((backward, kept))
    ahead, behind = crossed(ahead, 1, True), crossed(behind, 3, True)
    returned = lax.all_to_all(
        backward.reshape(64, 16, 256), DP, split_axis=0, concat_axis=0, tiled=True
    ).reshape(1024, 256)
    forth, back = call(
        add_relayed_body, [((2, 80, 1024), BF16)] * 2, (kept, ahead, behind), "add_relayed"
    )
    forth, back = crossed(forth, 1, True), crossed(back, 3, True)
    mid = call(
        add_four_body, [((80, 1024), BF16)] * 4, (kept, ahead, behind, forth, back), "add_four"
    )
    second = [mid[0]] + [crossed(mid[s], s, False) for s in (1, 2, 3)]
    returned, second[1] = lax.optimization_barrier((returned, second[1]))
    (columns,) = call(add_last_body, [((8, 80, 128), BF16)], second, "add_last")
    (grad_rows,) = call(
        rows_back, [((128, 1024), BF16)], (hist_blocks, owner, returned), "rows_back"
    )
    parts = lax.all_to_all(columns, "z", split_axis=0, concat_axis=0, tiled=True)
    (summed,) = call(add_eight_body, [((8, 80, 128), BF16)], (parts,), "add_eight")
    mine = lax.all_to_all(summed, "z", split_axis=0, concat_axis=0, tiled=True)
    lines = [mine] + [shift(mine, "y", 4, s) for s in (1, 2, 3)]
    paired = [shift(a, "c", 2, 1) for a in lines]
    g_in, g_out = call(
        place_body,
        [((256, 2048), F32), ((128, 1024), F32)],
        (*lines, *paired),
        "place",
        scratch=[((2, 4, 80, 1024), BF16)],
    )
    return layer_out[None], grad_rows[None], g_in, g_out


def solution(mesh):
    fine = Mesh(mesh.devices.reshape(8, 4, 2, 4), ("z", "y", "c", "x"))
    placed = (
        P("x", DP, None),
        P("x", DP, None),
        P("x", None),
        P("x", None),
        P("x", None),
        P("x", None),
    )
    return jax.shard_map(
        on_device,
        mesh=fine,
        in_specs=placed,
        out_specs=(P("x", DP, None), P("x", DP, None), P("x", None), P("x", None)),
        check_vma=False,
    )
```

```python
import functools

import jax
import jax.numpy as jnp
from jax import lax
from jax.experimental import pallas as pl
from jax.experimental.pallas import tpu as pltpu
from jax.sharding import Mesh, PartitionSpec as P

F32 = jnp.float32
BF16 = jnp.bfloat16
EPS = 1e-06
HEAD = 128
DP = ("z", "y", "c")
NN = (((1,), (0,)), ((), ()))
NT = (((1,), (1,)), ((), ()))
TN = (((0,), (0,)), ((), ()))
MIB = 1024 * 1024


def dot(a, b, dims=NN):
    return lax.dot_general(a, b, dims, preferred_element_type=F32)


def iota(shape, dim):
    return lax.broadcasted_iota(jnp.int32, shape, dim)


def call(body, outs, args, name, scratch=(), mib=12):
    return pl.pallas_call(
        body,
        out_shape=[jax.ShapeDtypeStruct(s, d) for s, d in outs],
        in_specs=[pl.BlockSpec(memory_space=pltpu.VMEM) for _ in args],
        out_specs=[pl.BlockSpec(memory_space=pltpu.VMEM) for _ in outs],
        scratch_shapes=[pltpu.VMEM(s, d) for s, d in scratch],
        compiler_params=pltpu.CompilerParams(vmem_limit_bytes=mib * MIB),
        name=name,
    )(*args)


def histories(blocks_ref, owners_ref):
    n_row = blocks_ref[...].astype(F32)
    o_row = owners_ref[...].astype(F32)
    count = n_row.shape[1]
    r, c = iota((count, count), 0), iota((count, count), 1)
    column = lambda cond, row: jnp.sum(jnp.where(cond, row, 0.0), axis=1, keepdims=True)
    n_col = column(r == c, n_row)
    o_col = column(r == c, o_row)
    start = column(c < r, n_row)
    same = o_col == o_row
    before_col = column((c < r) & same, n_row)
    before_row = jnp.sum(jnp.where((r < c) & same, n_col, 0.0), axis=0, keepdims=True)
    return n_row, o_row, n_col, o_col, start, before_col, before_row


def slots_of_rows(blocks_ref, owners_ref, count):
    _, _, n_col, o_col, start, before, _ = histories(blocks_ref, owners_ref)
    b = iota((n_col.shape[0], count), 1).astype(F32)
    inside = (start <= b) & (b < start + n_col)
    code = jnp.sum(jnp.where(inside, o_col * 4.0 + before - start, 0.0), axis=0, keepdims=True)
    return (code + b[:1]).astype(jnp.int32)


def entry_body(blocks_hbm, owners_hbm, x_hbm, w_in, w_out, out_ref, pack, blocks, owners, rows, sems):
    half = lax.axis_index("c")
    wide = pl.ds(pl.multiple_of(half * 1024, 1024), 1024)
    left = pl.ds(pl.multiple_of(half * 1024 // 2, 512), 512)
    copies = [
        pltpu.make_async_copy(a, b, sems.at[i])
        for i, (a, b) in enumerate(
            (
                (blocks_hbm, blocks),
                (owners_hbm, owners),
                (x_hbm, rows),
                (w_in.at[:, wide], pack.at[pl.ds(0, 256), :]),
                (w_out.at[pl.ds(0, 64), left], pack.at[pl.ds(256, 64), pl.ds(0, 512)]),
                (w_out.at[pl.ds(64, 64), left], pack.at[pl.ds(256, 64), pl.ds(512, 512)]),
            )
        )
    ]
    for copy in copies:
        copy.start()
    for copy in copies[:3]:
        copy.wait()
    code = slots_of_rows(blocks, owners, 128)
    row = iota((1024, 128), 0)
    total = None
    for j in range(4):
        pick = (row == code * 4 + j).astype(F32).astype(BF16)
        part = dot(pick, rows[:, j * 256 : (j + 1) * 256])
        total = part if total is None else total + part
    out_ref[...] = total.astype(BF16)
    for copy in copies[3:]:
        copy.wait()


def rows_back(blocks_ref, owners_ref, returned_ref, out_ref):
    code = slots_of_rows(blocks_ref, owners_ref, 128)
    eye = iota((128, 128), 0) == iota((128, 128), 1)
    column = jnp.sum(jnp.where(eye, code.astype(F32), 0.0), axis=1, keepdims=True).astype(jnp.int32)
    lane = iota((128, 1024), 1)
    for j in range(4):
        pick = (lane == column * 4 + j).astype(F32).astype(BF16)
        out_ref[:, j * 256 : (j + 1) * 256] = dot(pick, returned_ref[...]).astype(BF16)


def weights_of(x, half, refs):
    w_in, w_out, own, other = refs
    other_half = 1 - half

    def proj(k, is_own):
        if k == 0:
            h = half if is_own else other_half
            return w_in[:, pl.ds(pl.multiple_of(h * 1024, 1024), 1024)]
        left, right, top, low = own if is_own else other
        if k == 2:
            return jnp.concatenate([top[...], low[:96, :]], axis=0)
        return (left if k == 1 else right)[:256, :]

    def back(k, is_own):
        if k == 0:
            h = half if is_own else other_half
            return w_out[:, pl.ds(pl.multiple_of(h * 512, 512), 512)]
        left, right, top, low = own if is_own else other
        part = low[96:, :] if k == 2 else (left if k == 1 else right)[256:, :]
        return jnp.concatenate([part[:, :512], part[:, 512:]], axis=0)

    return proj, back


def order_of(half, sx, sy):
    return jnp.where(half == 0, sx, sy), jnp.where(half == 0, sy, sx)


ROWS = 256


def half_columns(half, width):
    return pl.ds(pl.multiple_of(half * width, width), width)


def forward_body(
    blocks_ref, owners_ref, arrived, cot, w_in, w_out, a1, a2, a3, a4, b1, b2, b3, b4,
    shared, owned, rstd, act, dsilu, hat, att_rstd, weights, dscore, w_full,
    wide, pre,
):
    x, y, c = lax.axis_index("x"), lax.axis_index("y"), lax.axis_index("c")
    me = (lax.axis_index("z") * 4 + y) * 2 + c
    proj, back = weights_of(x, c, (w_in, w_out, (a1, a2, a3, a4), (b1, b2, b3, b4)))
    halves = ((True, c), (False, 1 - c))

    for i in range(2):
        wide[i] = arrived[:, i * 128 : (i + 1) * 128].astype(F32)
    for s in range(4):
        for j in range(8):
            rows = wide.at[j % 2][pl.ds(s * 4 + j // 2, 64, stride=16), :]
            owned[s * 64 : (s + 1) * 64, j * 128 : (j + 1) * 128] = rows.astype(BF16)

    def norm_rows(rows):
        v = owned[rows, :].astype(F32)
        cen = v - jnp.sum(v, axis=1, keepdims=True) * (1.0 / 1024)
        rs = lax.rsqrt(jnp.sum(cen * cen, axis=1, keepdims=True) * (1.0 / 1024) + EPS)
        n = (cen * rs).astype(BF16)
        for j in range(4):
            shared[j, rows, :256] = n[:, j * 256 : (j + 1) * 256]
        rstd[rows, :] = jnp.broadcast_to(rs, (ROWS, 128))

    norm_rows(pl.ds(0, ROWS))
    right = cot[:, half_columns(1 - c, 512)]
    for j in range(4):
        shared[j, :, 384:] = right[:, j * 128 : (j + 1) * 128]
    for k in range(4):
        for is_own, h in halves:
            w_full[(x + 4 - k) % 4, :, half_columns(h, 512)] = back(k, is_own)

    for is_own, h in halves:
        total = None
        for k in range(4):
            part = dot(shared[(x + 4 - k) % 4, :, :256], proj(k, is_own))
            total = part if total is None else total + part
        pre[h] = total

    def activate(rows):
        for h in range(2):
            v = pre[h, rows, :]
            sig = jax.nn.sigmoid(v)
            act[h, rows, :] = (v * sig).astype(BF16)
            dsilu[h, rows, :] = sig * (1.0 + v * (1.0 - sig))

    activate(pl.ds(0, ROWS))

    n_row, o_row, n_col, o_col, _, before_col, before_row = histories(blocks_ref, owners_ref)
    mine = me.astype(F32)
    label = 1.0 + iota((64, 256), 0).astype(F32)
    at = iota((64, 256), 1).astype(F32)
    inside = (o_col == mine) & (at >= before_col * 64.0) & (at < (before_col + n_col) * 64.0)
    seg_row = jnp.sum(jnp.where(inside, label, 0.0), axis=0, keepdims=True)
    label = 1.0 + iota((256, 64), 1).astype(F32)
    at = iota((256, 64), 0).astype(F32)
    inside = (o_row == mine) & (at >= before_row * 64.0) & (at < (before_row + n_row) * 64.0)
    seg_col = jnp.sum(jnp.where(inside, label, 0.0), axis=1, keepdims=True)
    visible = (seg_row == seg_col) & (iota((256, 256), 1) <= iota((256, 256), 0)) & (seg_col > 0.0)
    mask = jnp.where(visible, 1.0 / 256.0, 0.0)

    scale = HEAD ** (-0.5)
    for h in range(4):
        lo, hi = h * HEAD, (h + 1) * HEAD
        s = dot(act[1, :, lo:hi], act[1, :, 512 + lo : 512 + hi], NT) * scale
        sig = jax.nn.sigmoid(s)
        w = (s * sig * mask).astype(BF16)
        weights[h] = w
        dscore[h] = (mask * scale) * (sig * (1.0 + s * (1.0 - sig)))
        hat[:, lo:hi] = dot(w, act[0, :, 512 + lo : 512 + hi])

    def mix_rows(rows):
        v = hat[rows, :]
        cen = v - jnp.sum(v, axis=1, keepdims=True) * (1.0 / 512)
        rs = lax.rsqrt(jnp.sum(cen * cen, axis=1, keepdims=True) * (1.0 / 512) + EPS)
        cen = cen * rs
        mixed = (act[0, rows, :512].astype(F32) * cen).astype(BF16)
        for h in range(4):
            shared[h, rows, 256:384] = mixed[:, h * HEAD : (h + 1) * HEAD]
        hat[rows, :] = cen
        att_rstd[rows, :] = jnp.broadcast_to(rs, (ROWS, 128))

    mix_rows(pl.ds(0, ROWS))


def backward_body(
    shared, owned, cot, act, dsilu, hat, att_rstd, weights, dscore, w_full,
    out, kept, sent, dpre, dmixed, datt,
):
    c = lax.axis_index("c")
    w_out = w_full[...].reshape(512, 1024)
    mixed = jnp.concatenate([shared[h, :, 256:384] for h in range(4)], axis=1)
    out[...] = (dot(mixed, w_out) + owned[...].astype(F32)).astype(BF16)
    dmixed[...] = dot(cot[...], w_out, NT).astype(BF16)

    def unmix_rows(rows):
        dm = dmixed[rows, :].astype(F32)
        n = hat[rows, :]
        du = (dm * n).astype(BF16).astype(F32)
        dpre[0, rows, :512] = (du * dsilu[0, rows, :512]).astype(BF16)
        dh = dm * act[0, rows, :512].astype(F32)
        m1 = jnp.sum(dh, axis=1, keepdims=True) * (1.0 / 512)
        m2 = jnp.sum(dh * n, axis=1, keepdims=True) * (1.0 / 512)
        datt[rows, :] = (att_rstd[rows, :1] * (dh - m1 - n * m2)).astype(BF16)

    unmix_rows(pl.ds(0, ROWS))

    for h in range(4):
        lo, hi = h * HEAD, (h + 1) * HEAD
        d_h = datt[:, lo:hi]
        dw = dot(d_h, act[0, :, 512 + lo : 512 + hi], NT).astype(BF16).astype(F32)
        ds = (dw * dscore[h]).astype(BF16)
        dv = dot(weights[h], d_h, TN).astype(BF16).astype(F32)
        dq = dot(ds, act[1, :, 512 + lo : 512 + hi]).astype(BF16).astype(F32)
        dk = dot(ds, act[1, :, lo:hi], TN).astype(BF16).astype(F32)
        dpre[0, :, 512 + lo : 512 + hi] = (dv * dsilu[0, :, 512 + lo : 512 + hi]).astype(BF16)
        dpre[1, :, lo:hi] = (dq * dsilu[1, :, lo:hi]).astype(BF16)
        dpre[1, :, 512 + lo : 512 + hi] = (dk * dsilu[1, :, 512 + lo : 512 + hi]).astype(BF16)
    kept[...] = dpre[c]
    sent[...] = dpre[1 - c]


def rest_body(
    shared, rstd, cot, kept, sent, w_in, a1, a2, a3, a4, b1, b2, b3, b4,
    outgoing, dnorm, wide,
):
    x, c = lax.axis_index("x"), lax.axis_index("c")
    proj, _ = weights_of(x, c, (w_in, None, (a1, a2, a3, a4), (b1, b2, b3, b4)))
    for k in range(4):
        total = dot(kept[...], proj(k, True), NT) + dot(sent[...], proj(k, False), NT)
        dnorm[(x + 4 - k) % 4] = total.astype(BF16)

    dn = jnp.concatenate([dnorm[j] for j in range(4)], axis=1).astype(F32)
    n = jnp.concatenate([shared[j, :, :256] for j in range(4)], axis=1).astype(F32)
    m1 = jnp.sum(dn, axis=1, keepdims=True) * (1.0 / 1024)
    m2 = jnp.sum(dn * n, axis=1, keepdims=True) * (1.0 / 1024)
    d = rstd[:, :1] * (dn - m1 - n * m2) + cot[...].astype(F32)
    for s in range(4):
        for j in range(8):
            part = d[s * 64 : (s + 1) * 64, j * 128 : (j + 1) * 128]
            wide.at[j % 2][pl.ds(s * 4 + j // 2, 64, stride=16), :] = part
    for i in range(2):
        outgoing[:, i * 128 : (i + 1) * 128] = wide[i].astype(BF16)


def sum_pair_body(shared, other, kept, received, cot, backward, ahead, behind, held_own, held):
    x, y, c = lax.axis_index("x"), lax.axis_index("y"), lax.axis_index("c")
    right = cot[:, half_columns(c, 512)]
    other_right = jnp.concatenate([other[j, :, 384:] for j in range(4)], axis=1)
    for sx in range(4):
        block = (x + sx) % 4
        d_in = dot(shared[block, :, :256], kept[...], TN) + dot(other[block, :, :256], received[...], TN)
        d_out = dot(shared[block, :, 256:384], right, TN) + dot(other[block, :, 256:384], other_right, TN)
        d_in, d_out = d_in.astype(BF16), d_out.astype(BF16)
        tail = jnp.concatenate([d_out[:64], d_out[64:]], axis=1)
        for m in range(4):
            if m < 3:
                rows = d_in[80 * m : 80 * m + 80]
            else:
                rows = jnp.concatenate([d_in[240:], tail], axis=0)
            first, second = order_of(c, sx, (m + 4 - y) % 4)
            held[first, second] = rows
    ahead[0] = held[2, :2]
    ahead[1] = held[1, 2:]
    behind[0] = held[2, 2:]
    behind[1] = held[3, :2]
    held_own[:4] = held[0]
    held_own[4:6] = held[1, :2]
    held_own[6:] = held[3, 2:]


def add_relayed_body(kept, ahead, behind, forth, back):
    forth[...] = (kept[4:6].astype(F32) + ahead[0].astype(F32)).astype(BF16)
    back[...] = (kept[6:].astype(F32) + behind[0].astype(F32)).astype(BF16)


def add_four_body(kept, ahead, behind, forth, back, *outs):
    for s in range(4):
        if s < 2:
            total = kept[s].astype(F32) + behind[1, s].astype(F32) + forth[s].astype(F32)
        else:
            total = kept[s].astype(F32) + ahead[1, s - 2].astype(F32) + back[s - 2].astype(F32)
        outs[s][...] = total.astype(BF16)


def add_last_body(a0, a1, a2, a3, out):
    total = a0[...].astype(F32) + a1[...].astype(F32) + a2[...].astype(F32) + a3[...].astype(F32)
    total = total.astype(BF16)
    for j in range(8):
        out[j] = total[:, j * 128 : (j + 1) * 128]


def add_eight_body(parts, out):
    total = parts[0].astype(F32)
    for i in range(1, 8):
        total = total + parts[i].astype(F32)
    total = total.astype(BF16)
    for i in range(8):
        out[i] = total


def place_body(o0, o1, o2, o3, t0, t1, t2, t3, g_in, g_out, rows):
    y, c = lax.axis_index("y"), lax.axis_index("c")
    for refs, h in (((o0, o1, o2, o3), c), ((t0, t1, t2, t3), 1 - c)):
        for s in range(4):
            m = (y + 4 - s) % 4
            for j in range(8):
                rows[h, m, :, j * 128 : (j + 1) * 128] = refs[s][j]
    factor = 1.0 / 256.0
    for h in range(2):
        for m in range(3):
            g_in[80 * m : 80 * m + 80, h * 1024 : (h + 1) * 1024] = rows[h, m].astype(F32) * factor
        last = rows[h, 3].astype(F32) * factor
        g_in[240:, h * 1024 : (h + 1) * 1024] = last[:16]
        g_out[:64, h * 512 : (h + 1) * 512] = last[16:, :512]
        g_out[64:, h * 512 : (h + 1) * 512] = last[16:, 512:]


def shift(a, axis, n, s):
    return lax.ppermute(a, axis, [(i, (i + s) % n) for i in range(n)])


def crossed(a, s, first):
    pairs = []
    for z in range(8):
        for y in range(4):
            for c in range(2):
                for x in range(4):
                    over_x = (c == 0) == first
                    ty, tx = (y, (x + s) % 4) if over_x else ((y + s) % 4, x)
                    at = lambda v, w: ((z * 4 + v) * 2 + c) * 4 + w
                    pairs.append((at(y, x), at(ty, tx)))
    return lax.ppermute(a, ("z", "y", "c", "x"), pairs)


def on_device(x_rows, cotangent, w_in, w_out, hist_blocks, owner):
    cot = cotangent[0]
    hbm = pl.BlockSpec(memory_space=pltpu.HBM)
    outgoing, pack = pl.pallas_call(
        entry_body,
        out_shape=[
            jax.ShapeDtypeStruct((1024, 256), BF16),
            jax.ShapeDtypeStruct((320, 1024), BF16),
        ],
        in_specs=[hbm] * 5,
        out_specs=[pl.BlockSpec(memory_space=pltpu.VMEM)] * 2,
        scratch_shapes=[
            pltpu.VMEM((1, 64), jnp.int32),
            pltpu.VMEM((1, 64), jnp.int32),
            pltpu.VMEM((128, 1024), BF16),
            pltpu.SemaphoreType.DMA((6,)),
        ],
        compiler_params=pltpu.CompilerParams(vmem_limit_bytes=60 * MIB),
        name="entry",
    )(hist_blocks, owner, x_rows[0], w_in, w_out)
    left, right = shift(pack, "x", 4, 1), shift(pack, "x", 4, 3)
    arrived = lax.all_to_all(
        outgoing.reshape(64, 16, 256), DP, split_axis=0, concat_axis=0, tiled=True
    ).reshape(1024, 256)
    own = [left, right, shift(left[:160], "x", 4, 1), shift(right[160:], "x", 4, 3)]
    weights = (w_in, w_out, *own, *[shift(a, "c", 2, 1) for a in own])
    shared, owned, rstd, act, dsilu, hat, att_rstd, scores, dscore, w_full = call(
        forward_body,
        [
            ((4, 256, 512), BF16),
            ((256, 1024), BF16),
            ((256, 128), F32),
            ((2, 256, 1024), BF16),
            ((2, 256, 1024), F32),
            ((256, 512), F32),
            ((256, 128), F32),
            ((4, 256, 256), BF16),
            ((4, 256, 256), F32),
            ((4, 128, 1024), BF16),
        ],
        (hist_blocks, owner, arrived, cot) + weights,
        "forward",
        scratch=[((2, 1024, 128), F32), ((2, 256, 1024), F32)],
        mib=20,
    )
    other = shift(shared, "c", 2, 1)
    layer_out, kept, sent = call(
        backward_body,
        [((256, 1024), BF16)] * 3,
        (shared, owned, cot, act, dsilu, hat, att_rstd, scores, dscore, w_full),
        "backward",
        scratch=[((2, 256, 1024), BF16), ((256, 512), BF16), ((256, 512), BF16)],
        mib=12,
    )
    received = shift(sent, "c", 2, 1)
    (backward,) = call(
        rest_body,
        [((1024, 256), BF16)],
        (shared, rstd, cot, kept, sent, w_in) + weights[2:],
        "rest",
        scratch=[((4, 256, 256), BF16), ((2, 1024, 128), F32)],
        mib=12,
    )
    ahead, behind, kept = call(
        sum_pair_body,
        [((2, 2, 80, 1024), BF16), ((2, 2, 80, 1024), BF16), ((8, 80, 1024), BF16)],
        (shared, other, kept, received, cot, backward),
        "sum_pair",
        scratch=[((4, 4, 80, 1024), BF16)],
        mib=12,
    )
    backward, kept = lax.optimization_barrier((backward, kept))
    ahead, behind = crossed(ahead, 1, True), crossed(behind, 3, True)
    returned = lax.all_to_all(
        backward.reshape(64, 16, 256), DP, split_axis=0, concat_axis=0, tiled=True
    ).reshape(1024, 256)
    forth, back = call(
        add_relayed_body, [((2, 80, 1024), BF16)] * 2, (kept, ahead, behind), "add_relayed"
    )
    forth, back = crossed(forth, 1, True), crossed(back, 3, True)
    mid = call(
        add_four_body, [((80, 1024), BF16)] * 4, (kept, ahead, behind, forth, back), "add_four"
    )
    second = [mid[0]] + [crossed(mid[s], s, False) for s in (1, 2, 3)]
    (grad_rows,) = call(
        rows_back, [((128, 1024), BF16)], (hist_blocks, owner, returned), "rows_back"
    )
    grad_rows, second[1] = lax.optimization_barrier((grad_rows, second[1]))
    (columns,) = call(add_last_body, [((8, 80, 128), BF16)], second, "add_last")
    parts = lax.all_to_all(columns, "z", split_axis=0, concat_axis=0, tiled=True)
    (summed,) = call(add_eight_body, [((8, 80, 128), BF16)], (parts,), "add_eight")
    mine = lax.all_to_all(summed, "z", split_axis=0, concat_axis=0, tiled=True)
    lines = [mine] + [shift(mine, "y", 4, s) for s in (1, 2, 3)]
    paired = [shift(a, "c", 2, 1) for a in lines]
    g_in, g_out = call(
        place_body,
        [((256, 2048), F32), ((128, 1024), F32)],
        (*lines, *paired),
        "place",
        scratch=[((2, 4, 80, 1024), BF16)],
    )
    return layer_out[None], grad_rows[None], g_in, g_out


def solution(mesh):
    fine = Mesh(mesh.devices.reshape(8, 4, 2, 4), ("z", "y", "c", "x"))
    placed = (
        P("x", DP, None),
        P("x", DP, None),
        P("x", None),
        P("x", None),
        P("x", None),
        P("x", None),
    )
    return jax.shard_map(
        on_device,
        mesh=fine,
        in_specs=placed,
        out_specs=(P("x", DP, None), P("x", DP, None), P("x", None), P("x", None)),
        check_vma=False,
    )
```

```python
import functools

import jax
import jax.numpy as jnp
from jax import lax
from jax.experimental import pallas as pl
from jax.experimental.pallas import tpu as pltpu
from jax.sharding import Mesh, PartitionSpec as P

F32 = jnp.float32
BF16 = jnp.bfloat16
EPS = 1e-06
HEAD = 128
Z = ("zh", "zl")
DP = ("zh", "zl", "y", "c")
NN = (((1,), (0,)), ((), ()))
NT = (((1,), (1,)), ((), ()))
TN = (((0,), (0,)), ((), ()))
MIB = 1024 * 1024


def dot(a, b, dims=NN):
    return lax.dot_general(a, b, dims, preferred_element_type=F32)


def iota(shape, dim):
    return lax.broadcasted_iota(jnp.int32, shape, dim)


def call(body, outs, args, name, scratch=(), mib=12):
    return pl.pallas_call(
        body,
        out_shape=[jax.ShapeDtypeStruct(s, d) for s, d in outs],
        in_specs=[pl.BlockSpec(memory_space=pltpu.VMEM) for _ in args],
        out_specs=[pl.BlockSpec(memory_space=pltpu.VMEM) for _ in outs],
        scratch_shapes=[pltpu.VMEM(s, d) for s, d in scratch],
        compiler_params=pltpu.CompilerParams(vmem_limit_bytes=mib * MIB),
        name=name,
    )(*args)


def half_columns(half, width):
    return pl.ds(pl.multiple_of(half * width, width), width)


def histories(blocks_ref, owners_ref):
    n_row = blocks_ref[...].astype(F32)
    o_row = owners_ref[...].astype(F32)
    count = n_row.shape[1]
    r, c = iota((count, count), 0), iota((count, count), 1)
    column = lambda cond, row: jnp.sum(jnp.where(cond, row, 0.0), axis=1, keepdims=True)
    n_col = column(r == c, n_row)
    o_col = column(r == c, o_row)
    start = column(c < r, n_row)
    same = o_col == o_row
    before_col = column((c < r) & same, n_row)
    before_row = jnp.sum(jnp.where((r < c) & same, n_col, 0.0), axis=0, keepdims=True)
    return n_row, o_row, n_col, o_col, start, before_col, before_row


def slots_of_rows(blocks_ref, owners_ref, count, core=0):
    _, _, n_col, o_col, start, before, _ = histories(blocks_ref, owners_ref)
    o_col = (o_col.astype(jnp.int32) ^ core).astype(F32)
    b = iota((n_col.shape[0], count), 1).astype(F32)
    inside = (start <= b) & (b < start + n_col)
    code = jnp.sum(jnp.where(inside, o_col * 4.0 + before - start, 0.0), axis=0, keepdims=True)
    return (code + b[:1]).astype(jnp.int32)


def pack_body(w_in, w_out, pack, sems):
    half = lax.axis_index("c")
    wide, narrow = half_columns(half, 1024), half_columns(half, 512)
    copies = [
        pltpu.make_async_copy(a, b, sems.at[i])
        for i, (a, b) in enumerate(
            (
                (w_in.at[:, wide], pack.at[pl.ds(0, 256), :]),
                (w_out.at[pl.ds(0, 64), narrow], pack.at[pl.ds(256, 64), pl.ds(0, 512)]),
                (w_out.at[pl.ds(64, 64), narrow], pack.at[pl.ds(256, 64), pl.ds(512, 512)]),
            )
        )
    ]
    for copy in copies:
        copy.start()
    for copy in copies:
        copy.wait()


def rows_out_body(blocks, owners, rows, out_ref):
    code = slots_of_rows(blocks, owners, 128)
    row = iota((1024, 128), 0)
    total = None
    for j in range(4):
        pick = (row == code * 4 + j).astype(F32).astype(BF16)
        part = dot(pick, rows[:, j * 256 : (j + 1) * 256])
        total = part if total is None else total + part
    out_ref[...] = total.astype(BF16)


def rows_back(blocks_ref, owners_ref, returned_ref, out_ref):
    code = slots_of_rows(blocks_ref, owners_ref, 128, lax.axis_index("c"))
    eye = iota((128, 128), 0) == iota((128, 128), 1)
    column = jnp.sum(jnp.where(eye, code.astype(F32), 0.0), axis=1, keepdims=True).astype(jnp.int32)
    lane = iota((128, 1024), 1)
    for j in range(4):
        pick = (lane == column * 4 + j).astype(F32).astype(BF16)
        out_ref[:, j * 256 : (j + 1) * 256] = dot(pick, returned_ref[...]).astype(BF16)


def weights_of(x, half, refs):
    w_in, w_out, own, other = refs
    other_half = 1 - half

    def proj(k, is_own):
        if k == 0:
            h = half if is_own else other_half
            return w_in[:, pl.ds(pl.multiple_of(h * 1024, 1024), 1024)]
        left, right, top, low = own if is_own else other
        if k == 2:
            return jnp.concatenate([top[...], low[:96, :]], axis=0)
        return (left if k == 1 else right)[:256, :]

    def back(k, is_own):
        if k == 0:
            h = half if is_own else other_half
            return w_out[:, pl.ds(pl.multiple_of(h * 512, 512), 512)]
        left, right, top, low = own if is_own else other
        part = low[96:, :] if k == 2 else (left if k == 1 else right)[256:, :]
        return jnp.concatenate([part[:, :512], part[:, 512:]], axis=0)

    return proj, back


def order_of(half, sx, sy):
    return jnp.where(half == 0, sx, sy), jnp.where(half == 0, sy, sx)


ROWS = 256


def forward_body(
    blocks_ref, owners_ref, arrived, cot, w_in, w_out, a1, a2, a3, a4, b1, b2, b3, b4,
    shared, owned, rstd, act, dsilu, hat, att_rstd, weights, dscore, w_full,
    wide, pre,
):
    x, y, c = lax.axis_index("x"), lax.axis_index("y"), lax.axis_index("c")
    me = ((lax.axis_index("zh") * 4 + lax.axis_index("zl")) * 4 + y) * 2 + c
    proj, back = weights_of(x, c, (w_in, w_out, (a1, a2, a3, a4), (b1, b2, b3, b4)))
    halves = ((True, c), (False, 1 - c))

    for i in range(2):
        wide[i] = arrived[:, i * 128 : (i + 1) * 128].astype(F32)
    for s in range(4):
        for j in range(8):
            rows = wide.at[j % 2][pl.ds(s * 4 + j // 2, 64, stride=16), :]
            owned[s * 64 : (s + 1) * 64, j * 128 : (j + 1) * 128] = rows.astype(BF16)

    def norm_rows(rows):
        v = owned[rows, :].astype(F32)
        cen = v - jnp.sum(v, axis=1, keepdims=True) * (1.0 / 1024)
        rs = lax.rsqrt(jnp.sum(cen * cen, axis=1, keepdims=True) * (1.0 / 1024) + EPS)
        n = (cen * rs).astype(BF16)
        for j in range(4):
            shared[j, rows, :256] = n[:, j * 256 : (j + 1) * 256]
        rstd[rows, :] = jnp.broadcast_to(rs, (ROWS, 128))

    norm_rows(pl.ds(0, ROWS))
    right = cot[:, half_columns(1 - c, 512)]
    for j in range(4):
        shared[j, :, 384:] = right[:, j * 128 : (j + 1) * 128]
    for k in range(4):
        for is_own, h in halves:
            w_full[(x + 4 - k) % 4, :, half_columns(h, 512)] = back(k, is_own)

    for is_own, h in halves:
        total = None
        for k in range(4):
            part = dot(shared[(x + 4 - k) % 4, :, :256], proj(k, is_own))
            total = part if total is None else total + part
        pre[h] = total

    def activate(rows):
        for h in range(2):
            v = pre[h, rows, :]
            sig = jax.nn.sigmoid(v)
            act[h, rows, :] = (v * sig).astype(BF16)
            dsilu[h, rows, :] = sig * (1.0 + v * (1.0 - sig))

    activate(pl.ds(0, ROWS))

    n_row, o_row, n_col, o_col, _, before_col, before_row = histories(blocks_ref, owners_ref)
    mine = me.astype(F32)
    label = 1.0 + iota((64, 256), 0).astype(F32)
    at = iota((64, 256), 1).astype(F32)
    inside = (o_col == mine) & (at >= before_col * 64.0) & (at < (before_col + n_col) * 64.0)
    seg_row = jnp.sum(jnp.where(inside, label, 0.0), axis=0, keepdims=True)
    label = 1.0 + iota((256, 64), 1).astype(F32)
    at = iota((256, 64), 0).astype(F32)
    inside = (o_row == mine) & (at >= before_row * 64.0) & (at < (before_row + n_row) * 64.0)
    seg_col = jnp.sum(jnp.where(inside, label, 0.0), axis=1, keepdims=True)
    visible = (seg_row == seg_col) & (iota((256, 256), 1) <= iota((256, 256), 0)) & (seg_col > 0.0)
    mask = jnp.where(visible, 1.0 / 256.0, 0.0)

    scale = HEAD ** (-0.5)
    for h in range(4):
        lo, hi = h * HEAD, (h + 1) * HEAD
        s = dot(act[1, :, lo:hi], act[1, :, 512 + lo : 512 + hi], NT) * scale
        sig = jax.nn.sigmoid(s)
        w = (s * sig * mask).astype(BF16)
        weights[h] = w
        dscore[h] = (mask * scale) * (sig * (1.0 + s * (1.0 - sig)))
        hat[:, lo:hi] = dot(w, act[0, :, 512 + lo : 512 + hi])

    def mix_rows(rows):
        v = hat[rows, :]
        cen = v - jnp.sum(v, axis=1, keepdims=True) * (1.0 / 512)
        rs = lax.rsqrt(jnp.sum(cen * cen, axis=1, keepdims=True) * (1.0 / 512) + EPS)
        cen = cen * rs
        mixed = (act[0, rows, :512].astype(F32) * cen).astype(BF16)
        for h in range(4):
            shared[h, rows, 256:384] = mixed[:, h * HEAD : (h + 1) * HEAD]
        hat[rows, :] = cen
        att_rstd[rows, :] = jnp.broadcast_to(rs, (ROWS, 128))

    mix_rows(pl.ds(0, ROWS))


def backward_body(
    shared, owned, cot, act, dsilu, hat, att_rstd, weights, dscore, w_full,
    out, kept, sent, dpre, dmixed, datt,
):
    c = lax.axis_index("c")
    w_out = w_full[...].reshape(512, 1024)
    mixed = jnp.concatenate([shared[h, :, 256:384] for h in range(4)], axis=1)
    out[...] = (dot(mixed, w_out) + owned[...].astype(F32)).astype(BF16)
    dmixed[...] = dot(cot[...], w_out, NT).astype(BF16)

    def unmix_rows(rows):
        dm = dmixed[rows, :].astype(F32)
        n = hat[rows, :]
        du = (dm * n).astype(BF16).astype(F32)
        dpre[0, rows, :512] = (du * dsilu[0, rows, :512]).astype(BF16)
        dh = dm * act[0, rows, :512].astype(F32)
        m1 = jnp.sum(dh, axis=1, keepdims=True) * (1.0 / 512)
        m2 = jnp.sum(dh * n, axis=1, keepdims=True) * (1.0 / 512)
        datt[rows, :] = (att_rstd[rows, :1] * (dh - m1 - n * m2)).astype(BF16)

    unmix_rows(pl.ds(0, ROWS))

    for h in range(4):
        lo, hi = h * HEAD, (h + 1) * HEAD
        d_h = datt[:, lo:hi]
        dw = dot(d_h, act[0, :, 512 + lo : 512 + hi], NT).astype(BF16).astype(F32)
        ds = (dw * dscore[h]).astype(BF16)
        dv = dot(weights[h], d_h, TN).astype(BF16).astype(F32)
        dq = dot(ds, act[1, :, 512 + lo : 512 + hi]).astype(BF16).astype(F32)
        dk = dot(ds, act[1, :, lo:hi], TN).astype(BF16).astype(F32)
        dpre[0, :, 512 + lo : 512 + hi] = (dv * dsilu[0, :, 512 + lo : 512 + hi]).astype(BF16)
        dpre[1, :, lo:hi] = (dq * dsilu[1, :, lo:hi]).astype(BF16)
        dpre[1, :, 512 + lo : 512 + hi] = (dk * dsilu[1, :, 512 + lo : 512 + hi]).astype(BF16)
    kept[...] = dpre[c]
    sent[...] = dpre[1 - c]


def rest_body(
    shared, rstd, cot, kept, sent, w_in, a1, a2, a3, a4, b1, b2, b3, b4,
    same, across, dnorm, wide,
):
    x, c = lax.axis_index("x"), lax.axis_index("c")
    proj, _ = weights_of(x, c, (w_in, None, (a1, a2, a3, a4), (b1, b2, b3, b4)))
    for k in range(4):
        total = dot(kept[...], proj(k, True), NT) + dot(sent[...], proj(k, False), NT)
        dnorm[(x + 4 - k) % 4] = total.astype(BF16)

    dn = jnp.concatenate([dnorm[j] for j in range(4)], axis=1).astype(F32)
    n = jnp.concatenate([shared[j, :, :256] for j in range(4)], axis=1).astype(F32)
    m1 = jnp.sum(dn, axis=1, keepdims=True) * (1.0 / 1024)
    m2 = jnp.sum(dn * n, axis=1, keepdims=True) * (1.0 / 1024)
    d = rstd[:, :1] * (dn - m1 - n * m2) + cot[...].astype(F32)
    for s in range(4):
        for j in range(8):
            part = d[s * 64 : (s + 1) * 64, j * 128 : (j + 1) * 128]
            wide.at[j % 2][pl.ds(s * 4 + j // 2, 64, stride=16), :] = part
    for out, side in ((same, c), (across, 1 - c)):
        for chip in range(32):
            rows = pl.ds(pl.multiple_of((chip * 2 + side) * 16, 16), 16)
            for i in range(2):
                out[chip, :, i * 128 : (i + 1) * 128] = wide.at[i][rows, :].astype(BF16)


def both_sides_body(same, across, out):
    out[:, :16, :] = same[...]
    out[:, 16:, :] = across[...]


def sum_pair_body(shared, other, kept, received, cot, same, ahead, behind, held_own, held):
    x, y, c = lax.axis_index("x"), lax.axis_index("y"), lax.axis_index("c")
    right = cot[:, half_columns(c, 512)]
    other_right = jnp.concatenate([other[j, :, 384:] for j in range(4)], axis=1)
    for sx in range(4):
        block = (x + sx) % 4
        d_in = dot(shared[block, :, :256], kept[...], TN) + dot(other[block, :, :256], received[...], TN)
        d_out = dot(shared[block, :, 256:384], right, TN) + dot(other[block, :, 256:384], other_right, TN)
        d_in, d_out = d_in.astype(BF16), d_out.astype(BF16)
        tail = jnp.concatenate([d_out[:64], d_out[64:]], axis=1)
        for m in range(4):
            if m < 3:
                rows = d_in[80 * m : 80 * m + 80]
            else:
                rows = jnp.concatenate([d_in[240:], tail], axis=0)
            first, second = order_of(c, sx, (m + 4 - y) % 4)
            held[first, second] = rows
    ahead[0] = held[2, :2]
    ahead[1] = held[1, 2:]
    behind[0] = held[2, 2:]
    behind[1] = held[3, :2]
    held_own[:4] = held[0]
    held_own[4:6] = held[1, :2]
    held_own[6:] = held[3, 2:]


def add_relayed_body(kept, ahead, behind, forth, back):
    forth[...] = (kept[4:6].astype(F32) + ahead[0].astype(F32)).astype(BF16)
    back[...] = (kept[6:].astype(F32) + behind[0].astype(F32)).astype(BF16)


def add_four_body(kept, ahead, behind, forth, back, *outs):
    for s in range(4):
        if s < 2:
            total = kept[s].astype(F32) + behind[1, s].astype(F32) + forth[s].astype(F32)
        else:
            total = kept[s].astype(F32) + ahead[1, s - 2].astype(F32) + back[s - 2].astype(F32)
        outs[s][...] = total.astype(BF16)


def add_last_body(a0, a1, a2, a3, *refs):
    outs, held = refs[:4], refs[4]
    zl = lax.axis_index("zl")
    total = a0[...].astype(F32) + a1[...].astype(F32) + a2[...].astype(F32) + a3[...].astype(F32)
    total = total.astype(BF16)
    for j in range(4):
        held[(j + 4 - zl) % 4] = total[:, j * 256 : (j + 1) * 256]
    for s in range(4):
        outs[s][...] = held[s]


def add_near_body(a0, a1, a2, a3, out):
    total = a0[...].astype(F32) + a1[...].astype(F32) + a2[...].astype(F32) + a3[...].astype(F32)
    total = total.astype(BF16)
    for i in range(8):
        out[i] = total


def join_body(parts, out):
    for j in range(4):
        total = parts[j].astype(F32) + parts[4 + j].astype(F32)
        out[:, j * 256 : (j + 1) * 256] = total.astype(BF16)


def place_body(o0, o1, o2, o3, t0, t1, t2, t3, g_in, g_out, rows):
    y, c = lax.axis_index("y"), lax.axis_index("c")
    for refs, h in (((o0, o1, o2, o3), c), ((t0, t1, t2, t3), 1 - c)):
        for s in range(4):
            rows[h, (y + 4 - s) % 4] = refs[s][...]
    factor = 1.0 / 256.0
    for h in range(2):
        for m in range(3):
            g_in[80 * m : 80 * m + 80, h * 1024 : (h + 1) * 1024] = rows[h, m].astype(F32) * factor
        last = rows[h, 3].astype(F32) * factor
        g_in[240:, h * 1024 : (h + 1) * 1024] = last[:16]
        g_out[:64, h * 512 : (h + 1) * 512] = last[16:, :512]
        g_out[64:, h * 512 : (h + 1) * 512] = last[16:, 512:]


def shift(a, axis, n, s):
    return lax.ppermute(a, axis, [(i, (i + s) % n) for i in range(n)])


def crossed(a, s, first):
    pairs = []
    for z in range(8):
        for y in range(4):
            for c in range(2):
                for x in range(4):
                    over_x = (c == 0) == first
                    ty, tx = (y, (x + s) % 4) if over_x else ((y + s) % 4, x)
                    at = lambda v, w: ((z * 4 + v) * 2 + c) * 4 + w
                    pairs.append((at(y, x), at(ty, tx)))
    return lax.ppermute(a, ("zh", "zl", "y", "c", "x"), pairs)


def on_device(x_rows, cotangent, w_in, w_out, hist_blocks, owner):
    cot = cotangent[0]
    pack = pl.pallas_call(
        pack_body,
        out_shape=jax.ShapeDtypeStruct((320, 1024), BF16),
        in_specs=[pl.BlockSpec(memory_space=pltpu.HBM)] * 2,
        out_specs=pl.BlockSpec(memory_space=pltpu.VMEM),
        scratch_shapes=[pltpu.SemaphoreType.DMA((3,))],
        compiler_params=pltpu.CompilerParams(vmem_limit_bytes=60 * MIB),
        name="pack",
    )(w_in, w_out)
    left, right = shift(pack, "x", 4, 1), shift(pack, "x", 4, 3)
    (outgoing,) = call(
        rows_out_body,
        [((1024, 256), BF16)],
        (hist_blocks, owner, x_rows[0]),
        "rows_out",
        mib=60,
    )
    arrived = lax.all_to_all(
        outgoing.reshape(64, 16, 256), DP, split_axis=0, concat_axis=0, tiled=True
    ).reshape(1024, 256)
    own = [left, right, shift(left[:160], "x", 4, 1), shift(right[160:], "x", 4, 3)]
    weights = (w_in, w_out, *own, *[shift(a, "c", 2, 1) for a in own])
    shared, owned, rstd, act, dsilu, hat, att_rstd, scores, dscore, w_full = call(
        forward_body,
        [
            ((4, 256, 512), BF16),
            ((256, 1024), BF16),
            ((256, 128), F32),
            ((2, 256, 1024), BF16),
            ((2, 256, 1024), F32),
            ((256, 512), F32),
            ((256, 128), F32),
            ((4, 256, 256), BF16),
            ((4, 256, 256), F32),
            ((4, 128, 1024), BF16),
        ],
        (hist_blocks, owner, arrived, cot) + weights,
        "forward",
        scratch=[((2, 1024, 128), F32), ((2, 256, 1024), F32)],
        mib=20,
    )
    other = shift(shared, "c", 2, 1)
    layer_out, kept, sent = call(
        backward_body,
        [((256, 1024), BF16)] * 3,
        (shared, owned, cot, act, dsilu, hat, att_rstd, scores, dscore, w_full),
        "backward",
        scratch=[((2, 256, 1024), BF16), ((256, 512), BF16), ((256, 512), BF16)],
        mib=12,
    )
    received = shift(sent, "c", 2, 1)
    same, across = call(
        rest_body,
        [((32, 16, 256), BF16)] * 2,
        (shared, rstd, cot, kept, sent, w_in) + weights[2:],
        "rest",
        scratch=[((4, 256, 256), BF16), ((2, 1024, 128), F32)],
        mib=12,
    )
    ahead, behind, kept = call(
        sum_pair_body,
        [((2, 2, 80, 1024), BF16), ((2, 2, 80, 1024), BF16), ((8, 80, 1024), BF16)],
        (shared, other, kept, received, cot, same),
        "sum_pair",
        scratch=[((4, 4, 80, 1024), BF16)],
        mib=12,
    )
    across = shift(across, "c", 2, 1)
    across, kept = lax.optimization_barrier((across, kept))
    (backward,) = call(both_sides_body, [((32, 32, 256), BF16)], (same, across), "both_sides")
    ahead, behind = crossed(ahead, 1, True), crossed(behind, 3, True)
    returned = lax.all_to_all(
        backward, ("zh", "zl", "y"), split_axis=0, concat_axis=0, tiled=True
    ).reshape(1024, 256)
    forth, back = call(
        add_relayed_body, [((2, 80, 1024), BF16)] * 2, (kept, ahead, behind), "add_relayed"
    )
    forth, back = crossed(forth, 1, True), crossed(back, 3, True)
    mid = call(
        add_four_body, [((80, 1024), BF16)] * 4, (kept, ahead, behind, forth, back), "add_four"
    )
    second = [mid[0]] + [crossed(mid[s], s, False) for s in (1, 2, 3)]
    (grad_rows,) = call(
        rows_back, [((128, 1024), BF16)], (hist_blocks, owner, returned), "rows_back"
    )
    grad_rows, second[1] = lax.optimization_barrier((grad_rows, second[1]))
    quarters = call(
        add_last_body,
        [((80, 256), BF16)] * 4,
        second,
        "add_last",
        scratch=[((4, 80, 256), BF16)],
    )
    near = [quarters[0]] + [shift(quarters[s], "zl", 4, s) for s in (1, 2, 3)]
    (summed,) = call(add_near_body, [((8, 80, 256), BF16)], near, "add_near")
    parts = lax.all_to_all(summed, Z, split_axis=0, concat_axis=0, tiled=True)
    (mine,) = call(join_body, [((80, 1024), BF16)], (parts,), "join")
    lines = [mine] + [shift(mine, "y", 4, s) for s in (1, 2, 3)]
    paired = [shift(a, "c", 2, 1) for a in lines]
    g_in, g_out = call(
        place_body,
        [((256, 2048), F32), ((128, 1024), F32)],
        (*lines, *paired),
        "place",
        scratch=[((2, 4, 80, 1024), BF16)],
    )
    return layer_out[None], grad_rows[None], g_in, g_out


def solution(mesh):
    fine = Mesh(mesh.devices.reshape(2, 4, 4, 2, 4), ("zh", "zl", "y", "c", "x"))
    placed = (
        P("x", DP, None),
        P("x", DP, None),
        P("x", None),
        P("x", None),
        P("x", None),
        P("x", None),
    )
    return jax.shard_map(
        on_device,
        mesh=fine,
        in_specs=placed,
        out_specs=(P("x", DP, None), P("x", DP, None), P("x", None), P("x", None)),
        check_vma=False,
    )
```

```python
import functools

import jax
import jax.numpy as jnp
from jax import lax
from jax.experimental import pallas as pl
from jax.experimental.pallas import tpu as pltpu
from jax.sharding import Mesh, PartitionSpec as P

F32 = jnp.float32
BF16 = jnp.bfloat16
EPS = 1e-06
HEAD = 128
Z = ("zh", "zl")
DP = ("zh", "zl", "y", "c")
NN = (((1,), (0,)), ((), ()))
NT = (((1,), (1,)), ((), ()))
TN = (((0,), (0,)), ((), ()))
MIB = 1024 * 1024


def dot(a, b, dims=NN):
    return lax.dot_general(a, b, dims, preferred_element_type=F32)


def iota(shape, dim):
    return lax.broadcasted_iota(jnp.int32, shape, dim)


def call(body, outs, args, name, scratch=(), mib=12):
    return pl.pallas_call(
        body,
        out_shape=[jax.ShapeDtypeStruct(s, d) for s, d in outs],
        in_specs=[pl.BlockSpec(memory_space=pltpu.VMEM) for _ in args],
        out_specs=[pl.BlockSpec(memory_space=pltpu.VMEM) for _ in outs],
        scratch_shapes=[pltpu.VMEM(s, d) for s, d in scratch],
        compiler_params=pltpu.CompilerParams(vmem_limit_bytes=mib * MIB),
        name=name,
    )(*args)


def half_columns(half, width):
    return pl.ds(pl.multiple_of(half * width, width), width)


def histories(blocks_ref, owners_ref):
    n_row = blocks_ref[...].astype(F32)
    o_row = owners_ref[...].astype(F32)
    count = n_row.shape[1]
    r, c = iota((count, count), 0), iota((count, count), 1)
    column = lambda cond, row: jnp.sum(jnp.where(cond, row, 0.0), axis=1, keepdims=True)
    n_col = column(r == c, n_row)
    o_col = column(r == c, o_row)
    start = column(c < r, n_row)
    same = o_col == o_row
    before_col = column((c < r) & same, n_row)
    before_row = jnp.sum(jnp.where((r < c) & same, n_col, 0.0), axis=0, keepdims=True)
    return n_row, o_row, n_col, o_col, start, before_col, before_row


def slots_of_rows(blocks_ref, owners_ref, count, core=0):
    _, _, n_col, o_col, start, before, _ = histories(blocks_ref, owners_ref)
    o_col = (o_col.astype(jnp.int32) ^ core).astype(F32)
    b = iota((n_col.shape[0], count), 1).astype(F32)
    inside = (start <= b) & (b < start + n_col)
    code = jnp.sum(jnp.where(inside, o_col * 4.0 + before - start, 0.0), axis=0, keepdims=True)
    return (code + b[:1]).astype(jnp.int32)


def pack_body(w_in, w_out, pack, sems):
    half = lax.axis_index("c")
    wide, narrow = half_columns(half, 1024), half_columns(half, 512)
    copies = [
        pltpu.make_async_copy(a, b, sems.at[i])
        for i, (a, b) in enumerate(
            (
                (w_in.at[:, wide], pack.at[pl.ds(0, 256), :]),
                (w_out.at[pl.ds(0, 64), narrow], pack.at[pl.ds(256, 64), pl.ds(0, 512)]),
                (w_out.at[pl.ds(64, 64), narrow], pack.at[pl.ds(256, 64), pl.ds(512, 512)]),
            )
        )
    ]
    for copy in copies:
        copy.start()
    for copy in copies:
        copy.wait()


def rows_out_body(blocks, owners, rows, out_ref):
    code = slots_of_rows(blocks, owners, 128)
    row = iota((1024, 128), 0)
    total = None
    for j in range(4):
        pick = (row == code * 4 + j).astype(F32).astype(BF16)
        part = dot(pick, rows[:, j * 256 : (j + 1) * 256])
        total = part if total is None else total + part
    out_ref[...] = total.astype(BF16)


def rows_back(blocks_ref, owners_ref, returned_ref, out_ref):
    code = slots_of_rows(blocks_ref, owners_ref, 128, lax.axis_index("c"))
    eye = iota((128, 128), 0) == iota((128, 128), 1)
    column = jnp.sum(jnp.where(eye, code.astype(F32), 0.0), axis=1, keepdims=True).astype(jnp.int32)
    lane = iota((128, 1024), 1)
    for j in range(4):
        pick = (lane == column * 4 + j).astype(F32).astype(BF16)
        out_ref[:, j * 256 : (j + 1) * 256] = dot(pick, returned_ref[...]).astype(BF16)


def weights_of(x, half, refs):
    w_in, w_out, own, other = refs
    other_half = 1 - half

    def proj(k, is_own):
        if k == 0:
            h = half if is_own else other_half
            return w_in[:, pl.ds(pl.multiple_of(h * 1024, 1024), 1024)]
        left, right, top, low = own if is_own else other
        if k == 2:
            return jnp.concatenate([top[...], low[:96, :]], axis=0)
        return (left if k == 1 else right)[:256, :]

    def back(k, is_own):
        if k == 0:
            h = half if is_own else other_half
            return w_out[:, pl.ds(pl.multiple_of(h * 512, 512), 512)]
        left, right, top, low = own if is_own else other
        part = low[96:, :] if k == 2 else (left if k == 1 else right)[256:, :]
        return jnp.concatenate([part[:, :512], part[:, 512:]], axis=0)

    return proj, back


def order_of(half, sx, sy):
    return jnp.where(half == 0, sx, sy), jnp.where(half == 0, sy, sx)


ROWS = 256


def forward_body(
    blocks_ref, owners_ref, arrived, cot, w_in, w_out, a1, a2, a3, a4, b1, b2, b3, b4,
    shared, owned, rstd, act, dsilu, hat, att_rstd, weights, dscore, w_full,
    wide, pre,
):
    x, y, c = lax.axis_index("x"), lax.axis_index("y"), lax.axis_index("c")
    me = ((lax.axis_index("zh") * 4 + lax.axis_index("zl")) * 4 + y) * 2 + c
    proj, back = weights_of(x, c, (w_in, w_out, (a1, a2, a3, a4), (b1, b2, b3, b4)))
    halves = ((True, c), (False, 1 - c))

    for i in range(2):
        wide[i] = arrived[:, i * 128 : (i + 1) * 128].astype(F32)
    for s in range(4):
        for j in range(8):
            rows = wide.at[j % 2][pl.ds(s * 4 + j // 2, 64, stride=16), :]
            owned[s * 64 : (s + 1) * 64, j * 128 : (j + 1) * 128] = rows.astype(BF16)

    def norm_rows(rows):
        v = owned[rows, :].astype(F32)
        cen = v - jnp.sum(v, axis=1, keepdims=True) * (1.0 / 1024)
        rs = lax.rsqrt(jnp.sum(cen * cen, axis=1, keepdims=True) * (1.0 / 1024) + EPS)
        n = (cen * rs).astype(BF16)
        for j in range(4):
            shared[j, rows, :256] = n[:, j * 256 : (j + 1) * 256]
        rstd[rows, :] = jnp.broadcast_to(rs, (ROWS, 128))

    norm_rows(pl.ds(0, ROWS))
    right = cot[:, half_columns(1 - c, 512)]
    for j in range(4):
        shared[j, :, 384:] = right[:, j * 128 : (j + 1) * 128]
    for k in range(4):
        for is_own, h in halves:
            w_full[(x + 4 - k) % 4, :, half_columns(h, 512)] = back(k, is_own)

    for is_own, h in halves:
        total = None
        for k in range(4):
            part = dot(shared[(x + 4 - k) % 4, :, :256], proj(k, is_own))
            total = part if total is None else total + part
        pre[h] = total

    def activate(rows):
        for h in range(2):
            v = pre[h, rows, :]
            sig = jax.nn.sigmoid(v)
            act[h, rows, :] = (v * sig).astype(BF16)
            dsilu[h, rows, :] = sig * (1.0 + v * (1.0 - sig))

    activate(pl.ds(0, ROWS))

    n_row, o_row, n_col, o_col, _, before_col, before_row = histories(blocks_ref, owners_ref)
    mine = me.astype(F32)
    label = 1.0 + iota((64, 256), 0).astype(F32)
    at = iota((64, 256), 1).astype(F32)
    inside = (o_col == mine) & (at >= before_col * 64.0) & (at < (before_col + n_col) * 64.0)
    seg_row = jnp.sum(jnp.where(inside, label, 0.0), axis=0, keepdims=True)
    label = 1.0 + iota((256, 64), 1).astype(F32)
    at = iota((256, 64), 0).astype(F32)
    inside = (o_row == mine) & (at >= before_row * 64.0) & (at < (before_row + n_row) * 64.0)
    seg_col = jnp.sum(jnp.where(inside, label, 0.0), axis=1, keepdims=True)
    visible = (seg_row == seg_col) & (iota((256, 256), 1) <= iota((256, 256), 0)) & (seg_col > 0.0)
    mask = jnp.where(visible, 1.0 / 256.0, 0.0)

    scale = HEAD ** (-0.5)
    for h in range(4):
        lo, hi = h * HEAD, (h + 1) * HEAD
        s = dot(act[1, :, lo:hi], act[1, :, 512 + lo : 512 + hi], NT) * scale
        sig = jax.nn.sigmoid(s)
        w = (s * sig * mask).astype(BF16)
        weights[h] = w
        dscore[h] = (mask * scale) * (sig * (1.0 + s * (1.0 - sig)))
        hat[:, lo:hi] = dot(w, act[0, :, 512 + lo : 512 + hi])

    def mix_rows(rows):
        v = hat[rows, :]
        cen = v - jnp.sum(v, axis=1, keepdims=True) * (1.0 / 512)
        rs = lax.rsqrt(jnp.sum(cen * cen, axis=1, keepdims=True) * (1.0 / 512) + EPS)
        cen = cen * rs
        mixed = (act[0, rows, :512].astype(F32) * cen).astype(BF16)
        for h in range(4):
            shared[h, rows, 256:384] = mixed[:, h * HEAD : (h + 1) * HEAD]
        hat[rows, :] = cen
        att_rstd[rows, :] = jnp.broadcast_to(rs, (ROWS, 128))

    mix_rows(pl.ds(0, ROWS))


def backward_body(
    shared, owned, cot, act, dsilu, hat, att_rstd, weights, dscore, w_full,
    out, kept, sent, dpre, dmixed, datt,
):
    c = lax.axis_index("c")
    w_out = w_full[...].reshape(512, 1024)
    mixed = jnp.concatenate([shared[h, :, 256:384] for h in range(4)], axis=1)
    out[...] = (dot(mixed, w_out) + owned[...].astype(F32)).astype(BF16)
    dmixed[...] = dot(cot[...], w_out, NT).astype(BF16)

    def unmix_rows(rows):
        dm = dmixed[rows, :].astype(F32)
        n = hat[rows, :]
        du = (dm * n).astype(BF16).astype(F32)
        dpre[0, rows, :512] = (du * dsilu[0, rows, :512]).astype(BF16)
        dh = dm * act[0, rows, :512].astype(F32)
        m1 = jnp.sum(dh, axis=1, keepdims=True) * (1.0 / 512)
        m2 = jnp.sum(dh * n, axis=1, keepdims=True) * (1.0 / 512)
        datt[rows, :] = (att_rstd[rows, :1] * (dh - m1 - n * m2)).astype(BF16)

    unmix_rows(pl.ds(0, ROWS))

    for h in range(4):
        lo, hi = h * HEAD, (h + 1) * HEAD
        d_h = datt[:, lo:hi]
        dw = dot(d_h, act[0, :, 512 + lo : 512 + hi], NT).astype(BF16).astype(F32)
        ds = (dw * dscore[h]).astype(BF16)
        dv = dot(weights[h], d_h, TN).astype(BF16).astype(F32)
        dq = dot(ds, act[1, :, 512 + lo : 512 + hi]).astype(BF16).astype(F32)
        dk = dot(ds, act[1, :, lo:hi], TN).astype(BF16).astype(F32)
        dpre[0, :, 512 + lo : 512 + hi] = (dv * dsilu[0, :, 512 + lo : 512 + hi]).astype(BF16)
        dpre[1, :, lo:hi] = (dq * dsilu[1, :, lo:hi]).astype(BF16)
        dpre[1, :, 512 + lo : 512 + hi] = (dk * dsilu[1, :, 512 + lo : 512 + hi]).astype(BF16)
    kept[...] = dpre[c]
    sent[...] = dpre[1 - c]


def layer_body(
    blocks_ref, owners_ref, arrived, cot, w_in, w_out, a1, a2, a3, a4, b1, b2, b3, b4,
    shared, rstd, out, kept, sent,
    owned, act, dsilu, hat, att_rstd, weights, dscore, w_full, wide, pre, dpre, dmixed, datt,
):
    forward_body(
        blocks_ref, owners_ref, arrived, cot, w_in, w_out, a1, a2, a3, a4, b1, b2, b3, b4,
        shared, owned, rstd, act, dsilu, hat, att_rstd, weights, dscore, w_full, wide, pre,
    )
    backward_body(
        shared, owned, cot, act, dsilu, hat, att_rstd, weights, dscore, w_full,
        out, kept, sent, dpre, dmixed, datt,
    )


def rest_body(
    shared, rstd, cot, kept, sent, w_in, a1, a2, a3, a4, b1, b2, b3, b4,
    same, across, dnorm, wide,
):
    x, c = lax.axis_index("x"), lax.axis_index("c")
    proj, _ = weights_of(x, c, (w_in, None, (a1, a2, a3, a4), (b1, b2, b3, b4)))
    for k in range(4):
        total = dot(kept[...], proj(k, True), NT) + dot(sent[...], proj(k, False), NT)
        dnorm[(x + 4 - k) % 4] = total.astype(BF16)

    dn = jnp.concatenate([dnorm[j] for j in range(4)], axis=1).astype(F32)
    n = jnp.concatenate([shared[j, :, :256] for j in range(4)], axis=1).astype(F32)
    m1 = jnp.sum(dn, axis=1, keepdims=True) * (1.0 / 1024)
    m2 = jnp.sum(dn * n, axis=1, keepdims=True) * (1.0 / 1024)
    d = rstd[:, :1] * (dn - m1 - n * m2) + cot[...].astype(F32)
    for s in range(4):
        for j in range(8):
            part = d[s * 64 : (s + 1) * 64, j * 128 : (j + 1) * 128]
            wide.at[j % 2][pl.ds(s * 4 + j // 2, 64, stride=16), :] = part
    for out, side in ((same, c), (across, 1 - c)):
        for chip in range(32):
            rows = pl.ds(pl.multiple_of((chip * 2 + side) * 16, 16), 16)
            for i in range(2):
                out[chip, :, i * 128 : (i + 1) * 128] = wide.at[i][rows, :].astype(BF16)


def both_sides_body(same, across, out):
    out[:, :16, :] = same[...]
    out[:, 16:, :] = across[...]


def sum_pair_body(shared, other, kept, received, cot, same, ahead, behind, held_own, held):
    x, y, c = lax.axis_index("x"), lax.axis_index("y"), lax.axis_index("c")
    right = cot[:, half_columns(c, 512)]
    other_right = jnp.concatenate([other[j, :, 384:] for j in range(4)], axis=1)
    for sx in range(4):
        block = (x + sx) % 4
        d_in = dot(shared[block, :, :256], kept[...], TN) + dot(other[block, :, :256], received[...], TN)
        d_out = dot(shared[block, :, 256:384], right, TN) + dot(other[block, :, 256:384], other_right, TN)
        d_in, d_out = d_in.astype(BF16), d_out.astype(BF16)
        tail = jnp.concatenate([d_out[:64], d_out[64:]], axis=1)
        for m in range(4):
            if m < 3:
                rows = d_in[80 * m : 80 * m + 80]
            else:
                rows = jnp.concatenate([d_in[240:], tail], axis=0)
            first, second = order_of(c, sx, (m + 4 - y) % 4)
            held[first, second] = rows
    ahead[0] = held[2, :2]
    ahead[1] = held[1, 2:]
    behind[0] = held[2, 2:]
    behind[1] = held[3, :2]
    held_own[:4] = held[0]
    held_own[4:6] = held[1, :2]
    held_own[6:] = held[3, 2:]


def add_relayed_body(kept, ahead, behind, forth, back):
    forth[...] = (kept[4:6].astype(F32) + ahead[0].astype(F32)).astype(BF16)
    back[...] = (kept[6:].astype(F32) + behind[0].astype(F32)).astype(BF16)


def add_four_body(kept, ahead, behind, forth, back, *outs):
    for s in range(4):
        if s < 2:
            total = kept[s].astype(F32) + behind[1, s].astype(F32) + forth[s].astype(F32)
        else:
            total = kept[s].astype(F32) + ahead[1, s - 2].astype(F32) + back[s - 2].astype(F32)
        outs[s][...] = total.astype(BF16)


def add_last_body(a0, a1, a2, a3, *refs):
    outs, held = refs[:4], refs[4]
    zl = lax.axis_index("zl")
    total = a0[...].astype(F32) + a1[...].astype(F32) + a2[...].astype(F32) + a3[...].astype(F32)
    total = total.astype(BF16)
    for j in range(4):
        held[(j + 4 - zl) % 4] = total[:, j * 256 : (j + 1) * 256]
    for s in range(4):
        outs[s][...] = held[s]


def add_near_body(a0, a1, a2, a3, out):
    total = a0[...].astype(F32) + a1[...].astype(F32) + a2[...].astype(F32) + a3[...].astype(F32)
    total = total.astype(BF16)
    for i in range(8):
        out[i] = total


def join_body(parts, out):
    for j in range(4):
        total = parts[j].astype(F32) + parts[4 + j].astype(F32)
        out[:, j * 256 : (j + 1) * 256] = total.astype(BF16)


def place_body(o0, o1, o2, o3, t0, t1, t2, t3, g_in, g_out, rows):
    y, c = lax.axis_index("y"), lax.axis_index("c")
    for refs, h in (((o0, o1, o2, o3), c), ((t0, t1, t2, t3), 1 - c)):
        for s in range(4):
            rows[h, (y + 4 - s) % 4] = refs[s][...]
    factor = 1.0 / 256.0
    for h in range(2):
        for m in range(3):
            g_in[80 * m : 80 * m + 80, h * 1024 : (h + 1) * 1024] = rows[h, m].astype(F32) * factor
        last = rows[h, 3].astype(F32) * factor
        g_in[240:, h * 1024 : (h + 1) * 1024] = last[:16]
        g_out[:64, h * 512 : (h + 1) * 512] = last[16:, :512]
        g_out[64:, h * 512 : (h + 1) * 512] = last[16:, 512:]


def shift(a, axis, n, s):
    return lax.ppermute(a, axis, [(i, (i + s) % n) for i in range(n)])


def crossed(a, s, first):
    pairs = []
    for z in range(8):
        for y in range(4):
            for c in range(2):
                for x in range(4):
                    over_x = (c == 0) == first
                    ty, tx = (y, (x + s) % 4) if over_x else ((y + s) % 4, x)
                    at = lambda v, w: ((z * 4 + v) * 2 + c) * 4 + w
                    pairs.append((at(y, x), at(ty, tx)))
    return lax.ppermute(a, ("zh", "zl", "y", "c", "x"), pairs)


def on_device(x_rows, cotangent, w_in, w_out, hist_blocks, owner):
    cot = cotangent[0]
    pack = pl.pallas_call(
        pack_body,
        out_shape=jax.ShapeDtypeStruct((320, 1024), BF16),
        in_specs=[pl.BlockSpec(memory_space=pltpu.HBM)] * 2,
        out_specs=pl.BlockSpec(memory_space=pltpu.VMEM),
        scratch_shapes=[pltpu.SemaphoreType.DMA((3,))],
        compiler_params=pltpu.CompilerParams(vmem_limit_bytes=60 * MIB),
        name="pack",
    )(w_in, w_out)
    left, right = shift(pack, "x", 4, 1), shift(pack, "x", 4, 3)
    (outgoing,) = call(
        rows_out_body,
        [((1024, 256), BF16)],
        (hist_blocks, owner, x_rows[0]),
        "rows_out",
        mib=60,
    )
    arrived = lax.all_to_all(
        outgoing.reshape(64, 16, 256), DP, split_axis=0, concat_axis=0, tiled=True
    ).reshape(1024, 256)
    own = [left, right, shift(left[:160], "x", 4, 1), shift(right[160:], "x", 4, 3)]
    weights = (w_in, w_out, *own, *[shift(a, "c", 2, 1) for a in own])
    shared, rstd, layer_out, kept, sent = call(
        layer_body,
        [
            ((4, 256, 512), BF16),
            ((256, 128), F32),
            ((256, 1024), BF16),
            ((256, 1024), BF16),
            ((256, 1024), BF16),
        ],
        (hist_blocks, owner, arrived, cot) + weights,
        "layer",
        scratch=[
            ((256, 1024), BF16),
            ((2, 256, 1024), BF16),
            ((2, 256, 1024), F32),
            ((256, 512), F32),
            ((256, 128), F32),
            ((4, 256, 256), BF16),
            ((4, 256, 256), F32),
            ((4, 128, 1024), BF16),
            ((2, 1024, 128), F32),
            ((2, 256, 1024), F32),
            ((2, 256, 1024), BF16),
            ((256, 512), BF16),
            ((256, 512), BF16),
        ],
        mib=28,
    )
    other = shift(shared, "c", 2, 1)
    received = shift(sent, "c", 2, 1)
    same, across = call(
        rest_body,
        [((32, 16, 256), BF16)] * 2,
        (shared, rstd, cot, kept, sent, w_in) + weights[2:],
        "rest",
        scratch=[((4, 256, 256), BF16), ((2, 1024, 128), F32)],
        mib=12,
    )
    ahead, behind, kept = call(
        sum_pair_body,
        [((2, 2, 80, 1024), BF16), ((2, 2, 80, 1024), BF16), ((8, 80, 1024), BF16)],
        (shared, other, kept, received, cot, same),
        "sum_pair",
        scratch=[((4, 4, 80, 1024), BF16)],
        mib=12,
    )
    across = shift(across, "c", 2, 1)
    across, kept = lax.optimization_barrier((across, kept))
    (backward,) = call(both_sides_body, [((32, 32, 256), BF16)], (same, across), "both_sides")
    ahead, behind = crossed(ahead, 1, True), crossed(behind, 3, True)
    returned = lax.all_to_all(
        backward, ("zh", "zl", "y"), split_axis=0, concat_axis=0, tiled=True
    ).reshape(1024, 256)
    forth, back = call(
        add_relayed_body, [((2, 80, 1024), BF16)] * 2, (kept, ahead, behind), "add_relayed"
    )
    forth, back = crossed(forth, 1, True), crossed(back, 3, True)
    mid = call(
        add_four_body, [((80, 1024), BF16)] * 4, (kept, ahead, behind, forth, back), "add_four"
    )
    second = [mid[0]] + [crossed(mid[s], s, False) for s in (1, 2, 3)]
    (grad_rows,) = call(
        rows_back, [((128, 1024), BF16)], (hist_blocks, owner, returned), "rows_back"
    )
    grad_rows, second[1] = lax.optimization_barrier((grad_rows, second[1]))
    quarters = call(
        add_last_body,
        [((80, 256), BF16)] * 4,
        second,
        "add_last",
        scratch=[((4, 80, 256), BF16)],
    )
    near = [quarters[0]] + [shift(quarters[s], "zl", 4, s) for s in (1, 2, 3)]
    (summed,) = call(add_near_body, [((8, 80, 256), BF16)], near, "add_near")
    parts = lax.all_to_all(summed, Z, split_axis=0, concat_axis=0, tiled=True)
    (mine,) = call(join_body, [((80, 1024), BF16)], (parts,), "join")
    lines = [mine] + [shift(mine, "y", 4, s) for s in (1, 2, 3)]
    paired = [shift(a, "c", 2, 1) for a in lines]
    g_in, g_out = call(
        place_body,
        [((256, 2048), F32), ((128, 1024), F32)],
        (*lines, *paired),
        "place",
        scratch=[((2, 4, 80, 1024), BF16)],
    )
    return layer_out[None], grad_rows[None], g_in, g_out


def solution(mesh):
    fine = Mesh(mesh.devices.reshape(2, 4, 4, 2, 4), ("zh", "zl", "y", "c", "x"))
    placed = (
        P("x", DP, None),
        P("x", DP, None),
        P("x", None),
        P("x", None),
        P("x", None),
        P("x", None),
    )
    return jax.shard_map(
        on_device,
        mesh=fine,
        in_specs=placed,
        out_specs=(P("x", DP, None), P("x", DP, None), P("x", None), P("x", None)),
        check_vma=False,
    )
```

```python
import functools

import jax
import jax.numpy as jnp
from jax import lax
from jax.experimental import pallas as pl
from jax.experimental.pallas import tpu as pltpu
from jax.sharding import Mesh, PartitionSpec as P

F32 = jnp.float32
BF16 = jnp.bfloat16
EPS = 1e-06
HEAD = 128
Z = ("zh", "zl")
DP = ("zh", "zl", "y", "c")
NN = (((1,), (0,)), ((), ()))
NT = (((1,), (1,)), ((), ()))
TN = (((0,), (0,)), ((), ()))
MIB = 1024 * 1024


def dot(a, b, dims=NN):
    return lax.dot_general(a, b, dims, preferred_element_type=F32)


def iota(shape, dim):
    return lax.broadcasted_iota(jnp.int32, shape, dim)


def call(body, outs, args, name, scratch=(), mib=12):
    return pl.pallas_call(
        body,
        out_shape=[jax.ShapeDtypeStruct(s, d) for s, d in outs],
        in_specs=[pl.BlockSpec(memory_space=pltpu.VMEM) for _ in args],
        out_specs=[pl.BlockSpec(memory_space=pltpu.VMEM) for _ in outs],
        scratch_shapes=[pltpu.VMEM(s, d) for s, d in scratch],
        compiler_params=pltpu.CompilerParams(vmem_limit_bytes=mib * MIB),
        name=name,
    )(*args)


def half_columns(half, width):
    return pl.ds(pl.multiple_of(half * width, width), width)


def histories(blocks_ref, owners_ref):
    n_row = blocks_ref[...].astype(F32)
    o_row = owners_ref[...].astype(F32)
    count = n_row.shape[1]
    r, c = iota((count, count), 0), iota((count, count), 1)
    column = lambda cond, row: jnp.sum(jnp.where(cond, row, 0.0), axis=1, keepdims=True)
    n_col = column(r == c, n_row)
    o_col = column(r == c, o_row)
    start = column(c < r, n_row)
    same = o_col == o_row
    before_col = column((c < r) & same, n_row)
    before_row = jnp.sum(jnp.where((r < c) & same, n_col, 0.0), axis=0, keepdims=True)
    return n_row, o_row, n_col, o_col, start, before_col, before_row


def slots_of_rows(blocks_ref, owners_ref, count, core=0):
    _, _, n_col, o_col, start, before, _ = histories(blocks_ref, owners_ref)
    o_col = (o_col.astype(jnp.int32) ^ core).astype(F32)
    b = iota((n_col.shape[0], count), 1).astype(F32)
    inside = (start <= b) & (b < start + n_col)
    code = jnp.sum(jnp.where(inside, o_col * 4.0 + before - start, 0.0), axis=0, keepdims=True)
    return (code + b[:1]).astype(jnp.int32)


def pack_body(w_in, w_out, pack, sems):
    half = lax.axis_index("c")
    wide, narrow = half_columns(half, 1024), half_columns(half, 512)
    copies = [
        pltpu.make_async_copy(a, b, sems.at[i])
        for i, (a, b) in enumerate(
            (
                (w_in.at[:, wide], pack.at[pl.ds(0, 256), :]),
                (w_out.at[pl.ds(0, 64), narrow], pack.at[pl.ds(256, 64), pl.ds(0, 512)]),
                (w_out.at[pl.ds(64, 64), narrow], pack.at[pl.ds(256, 64), pl.ds(512, 512)]),
            )
        )
    ]
    for copy in copies:
        copy.start()
    for copy in copies:
        copy.wait()


def rows_out_body(blocks, owners, rows, out_ref):
    code = slots_of_rows(blocks, owners, 128)
    row = iota((1024, 128), 0)
    total = None
    for j in range(4):
        pick = (row == code * 4 + j).astype(F32).astype(BF16)
        part = dot(pick, rows[:, j * 256 : (j + 1) * 256])
        total = part if total is None else total + part
    out_ref[...] = total.astype(BF16)


def rows_back(blocks_ref, owners_ref, returned_ref, out_ref):
    code = slots_of_rows(blocks_ref, owners_ref, 128, lax.axis_index("c"))
    eye = iota((128, 128), 0) == iota((128, 128), 1)
    column = jnp.sum(jnp.where(eye, code.astype(F32), 0.0), axis=1, keepdims=True).astype(jnp.int32)
    lane = iota((128, 1024), 1)
    for j in range(4):
        pick = (lane == column * 4 + j).astype(F32).astype(BF16)
        out_ref[:, j * 256 : (j + 1) * 256] = dot(pick, returned_ref[...]).astype(BF16)


def weights_of(x, half, refs):
    w_in, w_out, own, other = refs
    other_half = 1 - half

    def proj(k, is_own):
        if k == 0:
            h = half if is_own else other_half
            return w_in[:, pl.ds(pl.multiple_of(h * 1024, 1024), 1024)]
        left, right, top, low = own if is_own else other
        if k == 2:
            return jnp.concatenate([top[...], low[:96, :]], axis=0)
        return (left if k == 1 else right)[:256, :]

    def back(k, is_own):
        if k == 0:
            h = half if is_own else other_half
            return w_out[:, pl.ds(pl.multiple_of(h * 512, 512), 512)]
        left, right, top, low = own if is_own else other
        part = low[96:, :] if k == 2 else (left if k == 1 else right)[256:, :]
        return jnp.concatenate([part[:, :512], part[:, 512:]], axis=0)

    return proj, back


def order_of(half, sx, sy):
    return jnp.where(half == 0, sx, sy), jnp.where(half == 0, sy, sx)


ROWS = 256


def forward_body(
    blocks_ref, owners_ref, arrived, cot, w_in, w_out, a1, a2, a3, a4, b1, b2, b3, b4,
    shared, owned, rstd, act, dsilu, hat, att_rstd, weights, dscore, w_full,
    wide, pre, dmixed,
):
    x, y, c = lax.axis_index("x"), lax.axis_index("y"), lax.axis_index("c")
    me = ((lax.axis_index("zh") * 4 + lax.axis_index("zl")) * 4 + y) * 2 + c
    proj, back = weights_of(x, c, (w_in, w_out, (a1, a2, a3, a4), (b1, b2, b3, b4)))
    halves = ((True, c), (False, 1 - c))

    for i in range(2):
        wide[i] = arrived[:, i * 128 : (i + 1) * 128].astype(F32)
    for s in range(4):
        for j in range(8):
            rows = wide.at[j % 2][pl.ds(s * 4 + j // 2, 64, stride=16), :]
            owned[s * 64 : (s + 1) * 64, j * 128 : (j + 1) * 128] = rows.astype(BF16)

    def norm_rows(rows):
        v = owned[rows, :].astype(F32)
        cen = v - jnp.sum(v, axis=1, keepdims=True) * (1.0 / 1024)
        rs = lax.rsqrt(jnp.sum(cen * cen, axis=1, keepdims=True) * (1.0 / 1024) + EPS)
        n = (cen * rs).astype(BF16)
        for j in range(4):
            shared[j, rows, :256] = n[:, j * 256 : (j + 1) * 256]
        rstd[rows, :] = jnp.broadcast_to(rs, (ROWS, 128))

    norm_rows(pl.ds(0, ROWS))
    right = cot[:, half_columns(1 - c, 512)]
    for j in range(4):
        shared[j, :, 384:] = right[:, j * 128 : (j + 1) * 128]
    for k in range(4):
        for is_own, h in halves:
            w_full[(x + 4 - k) % 4, :, half_columns(h, 512)] = back(k, is_own)

    for is_own, h in halves:
        total = None
        for k in range(4):
            part = dot(shared[(x + 4 - k) % 4, :, :256], proj(k, is_own))
            total = part if total is None else total + part
        pre[h] = total

    def activate(rows):
        for h in range(2):
            v = pre[h, rows, :]
            sig = jax.nn.sigmoid(v)
            act[h, rows, :] = (v * sig).astype(BF16)
            dsilu[h, rows, :] = sig * (1.0 + v * (1.0 - sig))

    dmixed[...] = dot(cot[...], w_full[...].reshape(512, 1024), NT).astype(BF16)
    activate(pl.ds(0, ROWS))

    n_row, o_row, n_col, o_col, _, before_col, before_row = histories(blocks_ref, owners_ref)
    mine = me.astype(F32)
    label = 1.0 + iota((64, 256), 0).astype(F32)
    at = iota((64, 256), 1).astype(F32)
    inside = (o_col == mine) & (at >= before_col * 64.0) & (at < (before_col + n_col) * 64.0)
    seg_row = jnp.sum(jnp.where(inside, label, 0.0), axis=0, keepdims=True)
    label = 1.0 + iota((256, 64), 1).astype(F32)
    at = iota((256, 64), 0).astype(F32)
    inside = (o_row == mine) & (at >= before_row * 64.0) & (at < (before_row + n_row) * 64.0)
    seg_col = jnp.sum(jnp.where(inside, label, 0.0), axis=1, keepdims=True)
    visible = (seg_row == seg_col) & (iota((256, 256), 1) <= iota((256, 256), 0)) & (seg_col > 0.0)
    mask = jnp.where(visible, 1.0 / 256.0, 0.0)

    scale = HEAD ** (-0.5)
    for h in range(4):
        lo, hi = h * HEAD, (h + 1) * HEAD
        s = dot(act[1, :, lo:hi], act[1, :, 512 + lo : 512 + hi], NT) * scale
        sig = jax.nn.sigmoid(s)
        w = (s * sig * mask).astype(BF16)
        weights[h] = w
        dscore[h] = (mask * scale) * (sig * (1.0 + s * (1.0 - sig)))
        hat[:, lo:hi] = dot(w, act[0, :, 512 + lo : 512 + hi])

    def mix_rows(rows):
        v = hat[rows, :]
        cen = v - jnp.sum(v, axis=1, keepdims=True) * (1.0 / 512)
        rs = lax.rsqrt(jnp.sum(cen * cen, axis=1, keepdims=True) * (1.0 / 512) + EPS)
        cen = cen * rs
        mixed = (act[0, rows, :512].astype(F32) * cen).astype(BF16)
        for h in range(4):
            shared[h, rows, 256:384] = mixed[:, h * HEAD : (h + 1) * HEAD]
        hat[rows, :] = cen
        att_rstd[rows, :] = jnp.broadcast_to(rs, (ROWS, 128))

    mix_rows(pl.ds(0, ROWS))


def backward_body(
    shared, owned, cot, act, dsilu, hat, att_rstd, weights, dscore, w_full,
    out, kept, sent, dpre, dmixed, datt,
):
    c = lax.axis_index("c")
    w_out = w_full[...].reshape(512, 1024)
    mixed = jnp.concatenate([shared[h, :, 256:384] for h in range(4)], axis=1)
    out[...] = (dot(mixed, w_out) + owned[...].astype(F32)).astype(BF16)

    def unmix_rows(rows):
        dm = dmixed[rows, :].astype(F32)
        n = hat[rows, :]
        du = (dm * n).astype(BF16).astype(F32)
        dpre[0, rows, :512] = (du * dsilu[0, rows, :512]).astype(BF16)
        dh = dm * act[0, rows, :512].astype(F32)
        m1 = jnp.sum(dh, axis=1, keepdims=True) * (1.0 / 512)
        m2 = jnp.sum(dh * n, axis=1, keepdims=True) * (1.0 / 512)
        datt[rows, :] = (att_rstd[rows, :1] * (dh - m1 - n * m2)).astype(BF16)

    unmix_rows(pl.ds(0, ROWS))

    for h in range(4):
        lo, hi = h * HEAD, (h + 1) * HEAD
        d_h = datt[:, lo:hi]
        dw = dot(d_h, act[0, :, 512 + lo : 512 + hi], NT).astype(BF16).astype(F32)
        ds = (dw * dscore[h]).astype(BF16)
        dv = dot(weights[h], d_h, TN).astype(BF16).astype(F32)
        dq = dot(ds, act[1, :, 512 + lo : 512 + hi]).astype(BF16).astype(F32)
        dk = dot(ds, act[1, :, lo:hi], TN).astype(BF16).astype(F32)
        dpre[0, :, 512 + lo : 512 + hi] = (dv * dsilu[0, :, 512 + lo : 512 + hi]).astype(BF16)
        dpre[1, :, lo:hi] = (dq * dsilu[1, :, lo:hi]).astype(BF16)
        dpre[1, :, 512 + lo : 512 + hi] = (dk * dsilu[1, :, 512 + lo : 512 + hi]).astype(BF16)
    kept[...] = dpre[c]
    sent[...] = dpre[1 - c]


def layer_body(
    blocks_ref, owners_ref, arrived, cot, w_in, w_out, a1, a2, a3, a4, b1, b2, b3, b4,
    shared, rstd, out, kept, sent,
    owned, act, dsilu, hat, att_rstd, weights, dscore, w_full, wide, pre, dpre, dmixed, datt,
):
    forward_body(
        blocks_ref, owners_ref, arrived, cot, w_in, w_out, a1, a2, a3, a4, b1, b2, b3, b4,
        shared, owned, rstd, act, dsilu, hat, att_rstd, weights, dscore, w_full, wide, pre, dmixed,
    )
    backward_body(
        shared, owned, cot, act, dsilu, hat, att_rstd, weights, dscore, w_full,
        out, kept, sent, dpre, dmixed, datt,
    )


def rest_body(
    shared, rstd, cot, kept, sent, w_in, a1, a2, a3, a4, b1, b2, b3, b4,
    same, across, dnorm, wide,
):
    x, c = lax.axis_index("x"), lax.axis_index("c")
    proj, _ = weights_of(x, c, (w_in, None, (a1, a2, a3, a4), (b1, b2, b3, b4)))
    for k in range(4):
        total = dot(kept[...], proj(k, True), NT) + dot(sent[...], proj(k, False), NT)
        dnorm[(x + 4 - k) % 4] = total.astype(BF16)

    dn = jnp.concatenate([dnorm[j] for j in range(4)], axis=1).astype(F32)
    n = jnp.concatenate([shared[j, :, :256] for j in range(4)], axis=1).astype(F32)
    m1 = jnp.sum(dn, axis=1, keepdims=True) * (1.0 / 1024)
    m2 = jnp.sum(dn * n, axis=1, keepdims=True) * (1.0 / 1024)
    d = rstd[:, :1] * (dn - m1 - n * m2) + cot[...].astype(F32)
    for s in range(4):
        for j in range(8):
            part = d[s * 64 : (s + 1) * 64, j * 128 : (j + 1) * 128]
            wide.at[j % 2][pl.ds(s * 4 + j // 2, 64, stride=16), :] = part
    for out, side in ((same, c), (across, 1 - c)):
        for chip in range(32):
            rows = pl.ds(pl.multiple_of((chip * 2 + side) * 16, 16), 16)
            for i in range(2):
                out[chip, :, i * 128 : (i + 1) * 128] = wide.at[i][rows, :].astype(BF16)


def both_sides_body(same, across, out):
    out[:, :16, :] = same[...]
    out[:, 16:, :] = across[...]


def sum_pair_body(shared, other, kept, received, cot, same, ahead, behind, held_own, held):
    x, y, c = lax.axis_index("x"), lax.axis_index("y"), lax.axis_index("c")
    right = cot[:, half_columns(c, 512)]
    other_right = jnp.concatenate([other[j, :, 384:] for j in range(4)], axis=1)
    for sx in range(4):
        block = (x + sx) % 4
        d_in = dot(shared[block, :, :256], kept[...], TN) + dot(other[block, :, :256], received[...], TN)
        d_out = dot(shared[block, :, 256:384], right, TN) + dot(other[block, :, 256:384], other_right, TN)
        d_in, d_out = d_in.astype(BF16), d_out.astype(BF16)
        tail = jnp.concatenate([d_out[:64], d_out[64:]], axis=1)
        for m in range(4):
            if m < 3:
                rows = d_in[80 * m : 80 * m + 80]
            else:
                rows = jnp.concatenate([d_in[240:], tail], axis=0)
            first, second = order_of(c, sx, (m + 4 - y) % 4)
            held[first, second] = rows
    ahead[0] = held[2, :2]
    ahead[1] = held[1, 2:]
    behind[0] = held[2, 2:]
    behind[1] = held[3, :2]
    held_own[:4] = held[0]
    held_own[4:6] = held[1, :2]
    held_own[6:] = held[3, 2:]


def add_relayed_body(kept, ahead, behind, forth, back):
    forth[...] = (kept[4:6].astype(F32) + ahead[0].astype(F32)).astype(BF16)
    back[...] = (kept[6:].astype(F32) + behind[0].astype(F32)).astype(BF16)


def add_four_body(kept, ahead, behind, forth, back, *outs):
    for s in range(4):
        if s < 2:
            total = kept[s].astype(F32) + behind[1, s].astype(F32) + forth[s].astype(F32)
        else:
            total = kept[s].astype(F32) + ahead[1, s - 2].astype(F32) + back[s - 2].astype(F32)
        outs[s][...] = total.astype(BF16)


def add_last_body(a0, a1, a2, a3, *refs):
    outs, held = refs[:4], refs[4]
    zl = lax.axis_index("zl")
    total = a0[...].astype(F32) + a1[...].astype(F32) + a2[...].astype(F32) + a3[...].astype(F32)
    total = total.astype(BF16)
    for j in range(4):
        held[(j + 4 - zl) % 4] = total[:, j * 256 : (j + 1) * 256]
    for s in range(4):
        outs[s][...] = held[s]


def add_near_body(a0, a1, a2, a3, out):
    total = a0[...].astype(F32) + a1[...].astype(F32) + a2[...].astype(F32) + a3[...].astype(F32)
    total = total.astype(BF16)
    for i in range(8):
        out[i] = total


def join_body(parts, out):
    for j in range(4):
        total = parts[j].astype(F32) + parts[4 + j].astype(F32)
        out[:, j * 256 : (j + 1) * 256] = total.astype(BF16)


def place_body(o0, o1, o2, o3, t0, t1, t2, t3, g_in, g_out, rows):
    y, c = lax.axis_index("y"), lax.axis_index("c")
    for refs, h in (((o0, o1, o2, o3), c), ((t0, t1, t2, t3), 1 - c)):
        for s in range(4):
            rows[h, (y + 4 - s) % 4] = refs[s][...]
    factor = 1.0 / 256.0
    for h in range(2):
        for m in range(3):
            g_in[80 * m : 80 * m + 80, h * 1024 : (h + 1) * 1024] = rows[h, m].astype(F32) * factor
        last = rows[h, 3].astype(F32) * factor
        g_in[240:, h * 1024 : (h + 1) * 1024] = last[:16]
        g_out[:64, h * 512 : (h + 1) * 512] = last[16:, :512]
        g_out[64:, h * 512 : (h + 1) * 512] = last[16:, 512:]


def shift(a, axis, n, s):
    return lax.ppermute(a, axis, [(i, (i + s) % n) for i in range(n)])


def crossed(a, s, first):
    pairs = []
    for z in range(8):
        for y in range(4):
            for c in range(2):
                for x in range(4):
                    over_x = (c == 0) == first
                    ty, tx = (y, (x + s) % 4) if over_x else ((y + s) % 4, x)
                    at = lambda v, w: ((z * 4 + v) * 2 + c) * 4 + w
                    pairs.append((at(y, x), at(ty, tx)))
    return lax.ppermute(a, ("zh", "zl", "y", "c", "x"), pairs)


def on_device(x_rows, cotangent, w_in, w_out, hist_blocks, owner):
    cot = cotangent[0]
    pack = pl.pallas_call(
        pack_body,
        out_shape=jax.ShapeDtypeStruct((320, 1024), BF16),
        in_specs=[pl.BlockSpec(memory_space=pltpu.HBM)] * 2,
        out_specs=pl.BlockSpec(memory_space=pltpu.VMEM),
        scratch_shapes=[pltpu.SemaphoreType.DMA((3,))],
        compiler_params=pltpu.CompilerParams(vmem_limit_bytes=60 * MIB),
        name="pack",
    )(w_in, w_out)
    left, right = shift(pack, "x", 4, 1), shift(pack, "x", 4, 3)
    (outgoing,) = call(
        rows_out_body,
        [((1024, 256), BF16)],
        (hist_blocks, owner, x_rows[0]),
        "rows_out",
        mib=60,
    )
    arrived = lax.all_to_all(
        outgoing.reshape(64, 16, 256), DP, split_axis=0, concat_axis=0, tiled=True
    ).reshape(1024, 256)
    own = [left, right, shift(left[:160], "x", 4, 1), shift(right[160:], "x", 4, 3)]
    weights = (w_in, w_out, *own, *[shift(a, "c", 2, 1) for a in own])
    shared, rstd, layer_out, kept, sent = call(
        layer_body,
        [
            ((4, 256, 512), BF16),
            ((256, 128), F32),
            ((256, 1024), BF16),
            ((256, 1024), BF16),
            ((256, 1024), BF16),
        ],
        (hist_blocks, owner, arrived, cot) + weights,
        "layer",
        scratch=[
            ((256, 1024), BF16),
            ((2, 256, 1024), BF16),
            ((2, 256, 1024), F32),
            ((256, 512), F32),
            ((256, 128), F32),
            ((4, 256, 256), BF16),
            ((4, 256, 256), F32),
            ((4, 128, 1024), BF16),
            ((2, 1024, 128), F32),
            ((2, 256, 1024), F32),
            ((2, 256, 1024), BF16),
            ((256, 512), BF16),
            ((256, 512), BF16),
        ],
        mib=28,
    )
    other = shift(shared, "c", 2, 1)
    received = shift(sent, "c", 2, 1)
    same, across = call(
        rest_body,
        [((32, 16, 256), BF16)] * 2,
        (shared, rstd, cot, kept, sent, w_in) + weights[2:],
        "rest",
        scratch=[((4, 256, 256), BF16), ((2, 1024, 128), F32)],
        mib=12,
    )
    ahead, behind, kept = call(
        sum_pair_body,
        [((2, 2, 80, 1024), BF16), ((2, 2, 80, 1024), BF16), ((8, 80, 1024), BF16)],
        (shared, other, kept, received, cot, same),
        "sum_pair",
        scratch=[((4, 4, 80, 1024), BF16)],
        mib=12,
    )
    across = shift(across, "c", 2, 1)
    across, kept = lax.optimization_barrier((across, kept))
    (backward,) = call(both_sides_body, [((32, 32, 256), BF16)], (same, across), "both_sides")
    ahead, behind = crossed(ahead, 1, True), crossed(behind, 3, True)
    returned = lax.all_to_all(
        backward, ("zh", "zl", "y"), split_axis=0, concat_axis=0, tiled=True
    ).reshape(1024, 256)
    forth, back = call(
        add_relayed_body, [((2, 80, 1024), BF16)] * 2, (kept, ahead, behind), "add_relayed"
    )
    forth, back = crossed(forth, 1, True), crossed(back, 3, True)
    mid = call(
        add_four_body, [((80, 1024), BF16)] * 4, (kept, ahead, behind, forth, back), "add_four"
    )
    second = [mid[0]] + [crossed(mid[s], s, False) for s in (1, 2, 3)]
    (grad_rows,) = call(
        rows_back, [((128, 1024), BF16)], (hist_blocks, owner, returned), "rows_back"
    )
    grad_rows, second[1] = lax.optimization_barrier((grad_rows, second[1]))
    quarters = call(
        add_last_body,
        [((80, 256), BF16)] * 4,
        second,
        "add_last",
        scratch=[((4, 80, 256), BF16)],
    )
    near = [quarters[0]] + [shift(quarters[s], "zl", 4, s) for s in (1, 2, 3)]
    (summed,) = call(add_near_body, [((8, 80, 256), BF16)], near, "add_near")
    parts = lax.all_to_all(summed, Z, split_axis=0, concat_axis=0, tiled=True)
    (mine,) = call(join_body, [((80, 1024), BF16)], (parts,), "join")
    lines = [mine] + [shift(mine, "y", 4, s) for s in (1, 2, 3)]
    paired = [shift(a, "c", 2, 1) for a in lines]
    g_in, g_out = call(
        place_body,
        [((256, 2048), F32), ((128, 1024), F32)],
        (*lines, *paired),
        "place",
        scratch=[((2, 4, 80, 1024), BF16)],
    )
    return layer_out[None], grad_rows[None], g_in, g_out


def solution(mesh):
    fine = Mesh(mesh.devices.reshape(2, 4, 4, 2, 4), ("zh", "zl", "y", "c", "x"))
    placed = (
        P("x", DP, None),
        P("x", DP, None),
        P("x", None),
        P("x", None),
        P("x", None),
        P("x", None),
    )
    return jax.shard_map(
        on_device,
        mesh=fine,
        in_specs=placed,
        out_specs=(P("x", DP, None), P("x", DP, None), P("x", None), P("x", None)),
        check_vma=False,
    )
```
